128 devices in a mesh: row: 8 (over x, core), col: 16 (over z, y).
Axes of the slice: x: 4, y: 4, z: 4, core: 2. Of those that a mesh axis runs over, the one named last changes fastest.
Arguments:
- moisture: float32 [8, 512, 8192], P(None, 'row', 'col'), may hold values from 0.05 to 0.45
- lateral_cond: float32 [8, 512, 8192], P(None, 'row', 'col'), may hold values from 0.01 to 0.2
- vertical_cond: float32 [8, 512, 8192], P(None, 'row', 'col'), may hold values from 0.05 to 2
- rain: float32 [512, 8192], P('row', 'col'), may hold values from 0.01 to 0.5
- remap_cell: int32 [128, 128, 1024], P(('row', 'col')), may hold values from -1 to 32767, as said below
- remap_reach: int32 [128, 128, 1024], P(None, ('row', 'col')), may hold values from -1 to 2047, as said below
- travel_time: float32 [128, 2048], P('row', 'col'), may hold values from 0.03 to 0.8
- outflow_before: float32 [128, 2048], P('row', 'col'), may hold values from 0.5 to 1.5
- inflow_before: float32 [128, 2048], P('row', 'col'), may hold values from 0.5 to 1.5
- outlet_lane: int32 [8, 2048], P('row', 'col'), may hold values from 0 to 127
Outputs:
- moisture_new: float32 [8, 512, 8192], P(None, 'row', 'col')
- outflow_after: float32 [128, 2048], P('row', 'col')
- inflow_after: float32 [128, 2048], P('row', 'col')
The draws below stay inside these ranges and needn't reach their ends.
Inputs may be any that keep to these rules, and one draw needn't show every extreme that they name: `remap_cell`: in every list (source, destination) the live slots come first and the rest hold -1. A live slot names a cell of the sending device's 64 x 512 tile in row-major order; a cell may be named by several slots or by none. In every draw one destination receives 1024 live slots from every source, and every source fills all 1024 slots of one destination. `remap_reach`: -1 exactly where remap_cell is -1; else a reach q of the receiving device, q // 128 its segment and q % 128 its lane.
All inputs are finite; a program needn't handle non-finite values.
Results may differ from the reference program's by a relative error of at most 0.000086.
Values sent between devices are 32-bit elements; how exact they have to be, the bound alone decides.
A program may use at most 64 MiB of HBM per device.

```python
import math
import jax
import jax.numpy as jnp
from jax import lax

L = 8
TR = 64
TC = 512
SUB = 3
DEVICE_SEGMENTS = 16
DEVICE_CHAINS = 128
NR = 512
NC = 8192
SLOTS = 1024
SEGMENT_COUNT = 128
LANE_COUNT = 2048
N_ROW = 8
N_COL = 16
DEVICES = 128


def live_slots(key):
    random_keys = jax.random.split(key, 3)
    counts = jax.random.randint(random_keys[0], (DEVICES, DEVICES), 0, SLOTS + 1)
    heavy = jax.random.randint(random_keys[1], (), 0, DEVICES)
    extra = jax.random.randint(random_keys[2], (DEVICES,), 0, DEVICES)
    columns = jnp.arange(DEVICES, dtype=jnp.int32)
    full = (columns[None, :] == heavy) | (columns[None, :] == extra[:, None])
    counts = jnp.where(full, SLOTS, counts)
    return jnp.arange(SLOTS, dtype=jnp.int32)[None, None, :] < counts[:, :, None]


def draw_remap_cell(key, part):
    live = live_slots(key)
    key = jax.random.fold_in(key, 1)
    cells = jax.random.randint(key, (DEVICES, DEVICES, SLOTS), 0, TR * TC)
    return jnp.where(live, cells, -1).astype(jnp.int32)


def draw_remap_reach(key, part):
    live = live_slots(key)
    key = jax.random.fold_in(key, 2)
    reaches = jax.random.randint(key, (DEVICES, DEVICES, SLOTS), 0, DEVICE_SEGMENTS * DEVICE_CHAINS)
    return jnp.where(live, reaches, -1).astype(jnp.int32)


def logarithmic_range(key, array_shape, low, high):
    return jnp.exp(jax.random.uniform(key, array_shape, jnp.float32, math.log(low), math.log(high)))


def draw_travel_time(key, part):
    key = jax.random.fold_in(key, 7)
    random_keys = jax.random.split(key, 4)
    array_shape = (SEGMENT_COUNT, LANE_COUNT)
    base_value = logarithmic_range(random_keys[0], array_shape, 0.06, 0.4)
    multiplier = logarithmic_range(random_keys[1], (N_ROW, N_COL), 0.5, 2.0)
    multiplier = jnp.repeat(jnp.repeat(multiplier, DEVICE_SEGMENTS, 0), DEVICE_CHAINS, 1)
    pulse_rows = jax.random.randint(random_keys[2], (3,), 0, SEGMENT_COUNT)
    pulse_mask = jnp.any(jnp.arange(SEGMENT_COUNT)[:, None] == pulse_rows[None, :], 1)
    storm_pulse = logarithmic_range(random_keys[3], array_shape, 0.4, 0.8)
    return jnp.where(pulse_mask[:, None], storm_pulse, base_value * multiplier).astype(jnp.float32)


def with_ends(values, key, smallest, largest):
    shape = values.shape
    spot = [jax.random.randint(jax.random.fold_in(key, axis), (), 0, shape[axis]) for axis in range(len(shape))]
    values = values.at[tuple(spot)].set(smallest)
    longest = shape.index(max(shape))
    spot[longest] = (spot[longest] + 1) % shape[longest]
    return values.at[tuple(spot)].set(largest)


def shard_levels(stream_key, extent, pieces, low, high):
    level, own = 1.0, jax.random.fold_in(stream_key, 6)
    for dim, blocks in pieces:
        heights = jnp.exp(jax.random.uniform(jax.random.fold_in(own, dim), (blocks,), jnp.float32, low / len(pieces), high / len(pieces)))
        level = level * jnp.repeat(heights, extent[dim] // blocks).reshape([-1 if axis == dim else 1 for axis in range(len(extent))])
    return level


def setup_inputs(seed: int = 0) -> dict:
    seeds = jax.random.split(jax.random.key(seed), 11)
    return {
        "moisture": jnp.clip(0.05 + 0.39999999 * jax.random.uniform(seeds[0], (L, NR, NC), jnp.float32) ** shard_levels(seeds[0], (L, NR, NC), ((1, 8), (2, 16)), -0.2, 0.2), 0.05, 0.45),
        "lateral_cond": jnp.clip(jnp.exp(math.log(0.2) - 2.9957323 * jax.random.uniform(seeds[1], (L, NR, NC), jnp.float32) ** shard_levels(seeds[1], (L, NR, NC), ((1, 8), (2, 16)), -0.2, 0.2)), 0.01, 0.2),
        "vertical_cond": jnp.clip(jnp.exp(math.log(2.0) - 3.6888794 * jax.random.uniform(seeds[2], (L, NR, NC), jnp.float32) ** shard_levels(seeds[2], (L, NR, NC), ((1, 8), (2, 16)), -0.2, 0.2)), 0.05, 2.0),
        "rain": jnp.clip(jnp.exp(math.log(0.5) - 3.912023 * jax.random.uniform(seeds[3], (NR, NC), jnp.float32) ** shard_levels(seeds[3], (NR, NC), ((0, 8), (1, 16)), -0.2, 0.2)), 0.01, 0.5),
        "remap_cell": draw_remap_cell(jax.random.fold_in(seeds[10], 71), 0),
        "remap_reach": draw_remap_reach(jax.random.fold_in(seeds[10], 71), 0),
        "travel_time": draw_travel_time(jax.random.fold_in(seeds[10], 71), 0),
        "outflow_before": jnp.clip(0.5 + 1.0 * jax.random.uniform(seeds[7], (SEGMENT_COUNT, LANE_COUNT), jnp.float32) ** shard_levels(seeds[7], (SEGMENT_COUNT, LANE_COUNT), ((0, 8), (1, 16)), -0.2, 0.2), 0.5, 1.5),
        "inflow_before": jnp.clip(0.5 + 1.0 * jax.random.uniform(seeds[8], (SEGMENT_COUNT, LANE_COUNT), jnp.float32) ** shard_levels(seeds[8], (SEGMENT_COUNT, LANE_COUNT), ((0, 8), (1, 16)), -0.2, 0.2), 0.5, 1.5),
        "outlet_lane": with_ends(jax.random.randint(seeds[9], (N_ROW, LANE_COUNT), 0, DEVICE_CHAINS), jax.random.fold_in(seeds[9], 1), 0, DEVICE_CHAINS - 1).astype(jnp.int32),
    }


WEIGHT_X = 0.2
SIDEWAYS_FACTOR = 0.01


def lateral_moves(moist, cond):
    rows = moist.shape[1]
    cols = moist.shape[2]
    padded_cond = jnp.pad(cond, ((0, 0), (1, 1), (1, 1)))
    for step in range(SUB):
        padded_moist = jnp.pad(moist, ((0, 0), (1, 1), (1, 1)))
        total = jnp.zeros_like(moist)
        for row_off, col_off in ((0, 1), (2, 1), (1, 0), (1, 2)):
            near_moist = padded_moist[:, row_off:row_off + rows, col_off:col_off + cols]
            near_cond = padded_cond[:, row_off:row_off + rows, col_off:col_off + cols]
            face = 2.0 * cond * near_cond / (cond + near_cond)
            total = total + face * (near_moist - moist)
        moist = moist + total
    return moist


def vertical_solve(rhs, vcond):
    upper_list = []
    value_list = []
    for layer in range(L):
        diag = 1.0 + vcond[layer]
        right = rhs[layer]
        if layer > 0:
            above = vcond[layer - 1]
            diag = diag + above * (1.0 - upper_list[-1])
            right = right + above * value_list[-1]
        upper_list.append(vcond[layer] / diag)
        value_list.append(right / diag)
    result = [value_list[L - 1]]
    for layer in range(L - 2, -1, -1):
        result.insert(0, value_list[layer] + upper_list[layer] * result[0])
    return jnp.stack(result)


def reference(moisture, lateral_cond, vertical_cond, rain, remap_cell, remap_reach, travel_time, outflow_before, inflow_before, outlet_lane):
    surface = rain * (4.0 * moisture[0] * moisture[0])
    runoff = surface + vertical_cond[L - 1] * moisture[L - 1]
    tiles = runoff.reshape(N_ROW, TR, N_COL, TC).transpose(0, 2, 1, 3).reshape(DEVICES, TR * TC)
    cell_flat = remap_cell.reshape(DEVICES, DEVICES * SLOTS)
    picked = jnp.take_along_axis(tiles, jnp.maximum(cell_flat, 0), axis=1)
    sent = jnp.where(cell_flat >= 0, picked, jnp.float32(0.0))
    reach_count = DEVICE_SEGMENTS * DEVICE_CHAINS
    owner = jnp.arange(DEVICES, dtype=jnp.int32)[None, :, None] * reach_count
    reach_ids = owner + jnp.maximum(remap_reach, 0)
    accumulated_sum = jax.ops.segment_sum(sent.reshape(-1), reach_ids.reshape(-1), num_segments=DEVICES * reach_count)
    sideways_flux = SIDEWAYS_FACTOR * accumulated_sum.reshape(N_ROW, N_COL, DEVICE_SEGMENTS, DEVICE_CHAINS).transpose(0, 2, 1, 3).reshape(SEGMENT_COUNT, LANE_COUNT)

    denom = 1.0 + 2.0 * travel_time * (1.0 - WEIGHT_X)
    leading_coefficient = (1.0 - 2.0 * travel_time * WEIGHT_X) / denom
    coef_one = (1.0 + 2.0 * travel_time * WEIGHT_X) / denom
    coef_two = (2.0 * travel_time * (1.0 - WEIGHT_X) - 1.0) / denom
    remainder = coef_one * inflow_before + coef_two * outflow_before
    lane_cluster = (jnp.arange(LANE_COUNT, dtype=jnp.int32) // DEVICE_CHAINS) * DEVICE_CHAINS

    def block_advance(boundary, block):
        gain_rows, lat_rows, rest_rows, down_row = block

        def segment_step(upstream, row):
            gain_row, lat_row, rest_row = row
            inflow = upstream + lat_row
            flow = gain_row * inflow + rest_row
            return flow, (flow, inflow)

        final_entry, (outflow_values, inflow_values) = lax.scan(segment_step, boundary, (gain_rows, lat_rows, rest_rows))
        goal_reach = lane_cluster + down_row
        following_boundary = jnp.zeros((LANE_COUNT,), jnp.float32).at[goal_reach].add(final_entry)
        return following_boundary, (outflow_values, inflow_values)

    reshaped_array = (leading_coefficient.reshape(N_ROW, DEVICE_SEGMENTS, LANE_COUNT), sideways_flux.reshape(N_ROW, DEVICE_SEGMENTS, LANE_COUNT), remainder.reshape(N_ROW, DEVICE_SEGMENTS, LANE_COUNT), outlet_lane)
    discarded, (outflow_values, inflow_values) = lax.scan(block_advance, jnp.zeros((LANE_COUNT,), jnp.float32), reshaped_array)
    outflow_after = outflow_values.reshape(SEGMENT_COUNT, LANE_COUNT)
    inflow_after = inflow_values.reshape(SEGMENT_COUNT, LANE_COUNT)

    moved = lateral_moves(moisture, lateral_cond)
    rhs = jnp.concatenate([(moved[0] + (rain - surface))[None], moved[1:]], 0)
    moisture_new = vertical_solve(rhs, vertical_cond)
    return moisture_new, outflow_after, inflow_after
```

```python
import functools
import math

import jax
import jax.numpy as jnp
from jax import lax
from jax.experimental import pallas as pl
from jax.experimental.pallas import tpu as pltpu
from jax.sharding import PartitionSpec as P

SUB = 3
WEIGHT_X = 0.2
SIDEWAYS_FACTOR = 0.01

RUNOFF_LOW = 0.0025
RUNOFF_HIGH = 1.31
LOG_LOW = math.log(RUNOFF_LOW)
CODE_MAX = 65535.0
LOG_STEP = (math.log(RUNOFF_HIGH) - LOG_LOW) / CODE_MAX

UNROLL = 4
MESH = pl.DeviceIdType.MESH
NT = (((1,), (1,)), ((), ()))


def lookup_kernel(
    top_ref, bottom_ref, drain_ref, rain_ref, cell_ref, out_ref,
    cells, table, stage, looked, counts_vec, counts, chunks, sem, fetch_sem,
):
    dests, per = cells.shape[0:2]
    fetches = [
        pltpu.make_async_copy(
            cell_ref.at[0, :, j * 128 : (j + 1) * 128], cells.at[:, j, :], fetch_sem.at[j]
        )
        for j in range(per)
    ]
    for fetch in fetches:
        fetch.start()

    runoff = rain_ref[...] * (4.0 * top_ref[0] * top_ref[0]) + drain_ref[0] * bottom_ref[0]
    code = (jnp.log(runoff) - LOG_LOW) * (1.0 / LOG_STEP)
    code = jnp.clip(jnp.round(code), 0.0, CODE_MAX).astype(jnp.int32)
    rows = runoff.shape[0]
    for k in range(2):
        low = code[:, k * 128 : (k + 1) * 128]
        high = code[:, (k + 2) * 128 : (k + 3) * 128]
        table[k * rows : (k + 1) * rows, :] = low | (high << 16)

    out_ref[...] = jnp.zeros_like(out_ref)

    for fetch in fetches:
        fetch.wait()
    live = jnp.sum(jnp.where(cells[...] >= 0, 1, 0), axis=1)
    counts_vec[...] = jnp.transpose(live)[0:8, :]
    copy = pltpu.make_async_copy(counts_vec, counts, sem)
    copy.start()
    copy.wait()

    def enlist(d, total):
        for j in range(per):
            chunks[total + j] = d * per + j
        return total + counts[0, d]

    total = lax.fori_loop(0, dests, enlist, jnp.int32(0))
    for i in range(8 * UNROLL):
        chunks[total + i] = 0

    def step(g, carry):
        for u in range(UNROLL):
            for s in range(8):
                e = chunks[(g * UNROLL + u) * 8 + s]
                stage[u, s : s + 1, :] = cells[e >> 3, pl.ds(e & 7, 1), :]
        for u in range(UNROLL):
            cell = stage[u]
            lane = cell & 127
            word_row = ((cell >> 9) & 63) | ((cell >> 1) & 64)
            odd = [None, None]
            for t in range(2 * rows):
                row = jnp.broadcast_to(table[t : t + 1, :], (8, 128))
                got = jnp.take_along_axis(row, lane, axis=1, mode="promise_in_bounds")
                old = odd[t % 2]
                odd[t % 2] = got if old is None else jnp.where(word_row == t, got, old)
            word = jnp.where((word_row & 1) == 1, odd[1], odd[0])
            half = jnp.where(((cell >> 8) & 1) == 1, word >> 16, word) & 65535
            value = jnp.exp(half.astype(jnp.float32) * LOG_STEP + LOG_LOW)
            looked[u] = jnp.where(cell >= 0, value, 0.0)
        for u in range(UNROLL):
            for s in range(8):
                e = chunks[(g * UNROLL + u) * 8 + s]
                out_ref[e >> 3, pl.ds(e & 7, 1), :] = looked[u, s : s + 1, :]
        return carry

    lax.fori_loop(0, (total + (8 * UNROLL - 1)) // (8 * UNROLL), step, 0)


def look_up(moisture, vertical_cond, rain, remap_cell):
    layers, rows, cols = moisture.shape
    dests, slots = remap_cell.shape[1:]
    layer = lambda l: pl.BlockSpec((1, rows, cols), lambda i: (l, 0, 0))
    return pl.pallas_call(
        lookup_kernel,
        grid=(1,),
        in_specs=[
            layer(0),
            layer(layers - 1),
            layer(layers - 1),
            pl.BlockSpec((rows, cols), lambda i: (0, 0)),
            pl.BlockSpec(memory_space=pl.ANY),
        ],
        out_specs=pl.BlockSpec((dests, slots // 128, 128), lambda i: (0, 0, 0)),
        out_shape=jax.ShapeDtypeStruct((dests, slots // 128, 128), jnp.float32),
        scratch_shapes=[
            pltpu.VMEM((dests, slots // 128, 128), jnp.int32),
            pltpu.VMEM((2 * rows, 128), jnp.int32),
            pltpu.VMEM((UNROLL, 8, 128), jnp.int32),
            pltpu.VMEM((UNROLL, 8, 128), jnp.float32),
            pltpu.VMEM((8, dests), jnp.int32),
            pltpu.SMEM((8, dests), jnp.int32),
            pltpu.SMEM((dests * (slots // 128) + 8 * UNROLL + 8,), jnp.int32),
            pltpu.SemaphoreType.DMA,
            pltpu.SemaphoreType.DMA((slots // 128,)),
        ],
        compiler_params=pltpu.CompilerParams(vmem_limit_bytes=24 * 1024 * 1024),
        name="look_up",
    )(moisture, moisture, vertical_cond, rain, remap_cell)


GROUP = 8
HALF_BINS = 64


def bf16_split(x):
    head = x.astype(jnp.bfloat16)
    return head, (x - head.astype(jnp.float32)).astype(jnp.bfloat16)


def step_kernel(
    moist_ref, cond_ref, vert_ref, rain_ref, sent_ref, reach_ref,
    travel_ref, out_before_ref, in_before_ref, outlet_ref,
    new_ref, flow_ref, inflow_ref,
    wet, face, moved, below, above, pack_left, pack_right, from_right, from_left,
    arrived, leave, met, boundary,
    send_sem, recv_sem, row_send, row_recv, col_send, col_recv, own_sem, leave_send, leave_recv,
):
    n_row, n_col = lax.axis_size("row"), lax.axis_size("col")
    devices = n_row * n_col
    my_row, my_col = lax.axis_index("row"), lax.axis_index("col")
    me = my_row * n_col + my_col
    layers, rows, cols = moist_ref.shape
    height, width = rows + 8, cols + 128

    barrier = pltpu.get_barrier_semaphore()

    def greet(k, carry):
        other = lax.rem(me + k, devices)
        pl.semaphore_signal(
            barrier, inc=1, device_id=(other // n_col, lax.rem(other, n_col)), device_id_type=MESH
        )
        return carry

    lax.fori_loop(1, devices, greet, 0)
    pl.semaphore_wait(barrier, devices - 1)

    def row_copy(which, up):
        source = (moist_ref, cond_ref)[which]
        slot = 2 * which + (0 if up else 1)
        rows_out = source.at[:, 0:8, :] if up else source.at[:, rows - 8 : rows, :]
        place = below if up else above
        return pltpu.make_async_remote_copy(
            src_ref=rows_out,
            dst_ref=place.at[which],
            send_sem=row_send.at[slot],
            recv_sem=row_recv.at[slot],
            device_id=(my_row - 1 if up else my_row + 1, my_col),
            device_id_type=MESH,
        )

    has_up, has_down = my_row > 0, my_row < n_row - 1
    has_left, has_right = my_col > 0, my_col < n_col - 1

    @pl.when(has_up)
    def _():
        row_copy(0, True).start()
        row_copy(1, True).start()

    @pl.when(has_down)
    def _():
        row_copy(0, False).start()
        row_copy(1, False).start()

    def list_copy(k):
        other = lax.rem(me + k, devices)
        return pltpu.make_async_remote_copy(
            src_ref=sent_ref.at[other],
            dst_ref=arrived.at[k],
            send_sem=send_sem.at[k],
            recv_sem=recv_sem.at[k],
            device_id=(other // n_col, lax.rem(other, n_col)),
            device_id_type=MESH,
        )

    def send_list(k, carry):
        list_copy(k).start()
        return carry

    lax.fori_loop(1, devices, send_list, 0)
    own = pltpu.make_async_copy(sent_ref.at[me], arrived.at[0], own_sem)
    own.start()

    def extend(l, carry):
        wet[l, 0:rows, 0:cols] = moist_ref[l]
        face[l, 0:rows, 0:cols] = cond_ref[l]
        return carry

    lax.fori_loop(0, layers, extend, 0)
    sub = lax.broadcasted_iota(jnp.int32, (layers, 8, cols), 1)
    wet[:, rows:height, 0:cols] = jnp.zeros((layers, 8, cols), jnp.float32)
    face[:, rows:height, 0:cols] = jnp.zeros((layers, 8, cols), jnp.float32)

    @pl.when(has_down)
    def _():
        row_copy(0, True).wait_recv()
        row_copy(1, True).wait_recv()
        wet[:, rows:height, 0:cols] = jnp.where(sub < SUB, below[0], 0.0)
        face[:, rows:height, 0:cols] = jnp.where(sub < SUB, below[1], 0.0)

    @pl.when(has_up)
    def _():
        row_copy(0, False).wait_recv()
        row_copy(1, False).wait_recv()
        wet[:, rows:height, 0:cols] = jnp.where(sub >= 8 - SUB, above[0], wet[:, rows:height, 0:cols])
        face[:, rows:height, 0:cols] = jnp.where(sub >= 8 - SUB, above[1], face[:, rows:height, 0:cols])

    lane = lax.broadcasted_iota(jnp.int32, (height, 128), 1)
    left_pack = jnp.zeros((height, 128), jnp.float32)
    right_pack = jnp.zeros((height, 128), jnp.float32)
    for p in range(2 * layers):
        source = wet if p < layers else face
        here = (lane >= SUB * p) & (lane < SUB * (p + 1))
        first = source[p % layers, :, 0:128]
        last = source[p % layers, :, cols - 128 : cols]
        left_pack = jnp.where(here, pltpu.roll(first, SUB * p, 1) if p else first, left_pack)
        right_pack = jnp.where(here, pltpu.roll(last, SUB * p + SUB, 1), right_pack)
    pack_left[...] = left_pack
    pack_right[...] = right_pack

    def col_copy(left):
        return pltpu.make_async_remote_copy(
            src_ref=pack_left if left else pack_right,
            dst_ref=from_right if left else from_left,
            send_sem=col_send.at[0 if left else 1],
            recv_sem=col_recv.at[0 if left else 1],
            device_id=(my_row, my_col - 1 if left else my_col + 1),
            device_id_type=MESH,
        )

    @pl.when(has_left)
    def _():
        col_copy(True).start()

    @pl.when(has_right)
    def _():
        col_copy(False).start()

    travel = travel_ref[...]
    denom = 1.0 / (1.0 + 2.0 * travel * (1.0 - WEIGHT_X))
    gain = (1.0 - 2.0 * travel * WEIGHT_X) * denom
    rest = (1.0 + 2.0 * travel * WEIGHT_X) * denom * in_before_ref[...]
    rest += (2.0 * travel * (1.0 - WEIGHT_X) - 1.0) * denom * out_before_ref[...]

    wet[:, :, cols:width] = jnp.zeros((layers, height, 128), jnp.float32)
    face[:, :, cols:width] = jnp.zeros((layers, height, 128), jnp.float32)

    @pl.when(has_right)
    def _():
        col_copy(True).wait_recv()
        packed = from_right[...]
        for p in range(2 * layers):
            target = wet if p < layers else face
            part = pltpu.roll(packed, 128 - SUB * p, 1) if p else packed
            target[p % layers, :, cols:width] = jnp.where(lane < SUB, part, 0.0)

    @pl.when(has_left)
    def _():
        col_copy(False).wait_recv()
        packed = from_left[...]
        for p in range(2 * layers):
            target = wet if p < layers else face
            part = pltpu.roll(packed, 128 - SUB - SUB * p, 1)
            target[p % layers, :, cols:width] = jnp.where(
                lane >= 128 - SUB, part, target[p % layers, :, cols:width]
            )

    def lateral(l, carry):
        m, c = wet[l], face[l]
        down, right = pltpu.roll(c, height - 1, 0), pltpu.roll(c, width - 1, 1)
        face_down = 2.0 * c * down / jnp.maximum(c + down, 1e-30)
        face_right = 2.0 * c * right / jnp.maximum(c + right, 1e-30)
        for _ in range(SUB):
            flux_down = face_down * (pltpu.roll(m, height - 1, 0) - m)
            flux_right = face_right * (pltpu.roll(m, width - 1, 1) - m)
            m = m + (
                (flux_down - pltpu.roll(flux_down, 1, 0))
                + (flux_right - pltpu.roll(flux_right, 1, 1))
            )
        moved[l] = m[0:rows, 0:cols]
        return carry

    lax.fori_loop(0, layers, lateral, 0)

    own.wait()
    base = lax.broadcasted_iota(jnp.int32, (16, 1024), 0).astype(jnp.float32).astype(jnp.bfloat16)
    zero = jnp.zeros((16, 1024), jnp.bfloat16)
    one = jnp.ones((16, 1024), jnp.bfloat16)

    def spread(x):
        flat = jnp.concatenate([x[j : j + 1] for j in range(8)], 1)
        return jnp.broadcast_to(flat, (16, 1024))

    def add_up(g, acc):
        for u in range(GROUP):
            k = g * GROUP + u

            @pl.when(k > 0)
            def _():
                list_copy(k).wait()

        for u in range(GROUP):
            k = g * GROUP + u
            source = lax.rem(me - k + devices, devices)
            q = reach_ref[source]
            side = (q >> 7) + 16 * ((q >> 6) & 1)
            a = spread(side.astype(jnp.float32)).astype(jnp.bfloat16)
            b = spread((q & 63).astype(jnp.float32)).astype(jnp.bfloat16)
            head, tail = bf16_split(spread(arrived[k]))
            hits = [base + jnp.bfloat16(16 * t) == a for t in range(2)]
            values = jnp.concatenate(
                [jnp.where(h, head, zero) for h in hits] + [jnp.where(h, tail, zero) for h in hits], 0
            )
            places = jnp.concatenate(
                [jnp.where(base + jnp.bfloat16(16 * t) == b, one, zero) for t in range(4)], 0
            )
            acc = acc + lax.dot_general(values, places, NT, preferred_element_type=jnp.float32)
        return acc

    bins = lax.fori_loop(
        0, devices // GROUP, add_up, jnp.zeros((64, HALF_BINS), jnp.float32)
    )
    bins = SIDEWAYS_FACTOR * (bins[0:32] + bins[32:64])
    lateral_flow = jnp.concatenate([bins[0:16], bins[16:32]], 1)

    segments = lateral_flow.shape[0]
    offset_term = gain * lateral_flow + rest
    gains, offsets = [gain[0:1]], [offset_term[0:1]]
    for i in range(1, segments):
        g = gain[i : i + 1]
        gains.append(g * gains[-1])
        offsets.append(g * offsets[-1] + offset_term[i : i + 1])

    leave[0:1] = gains[-1]
    leave[1:2] = offsets[-1]
    leave[2:3] = outlet_ref[...].astype(jnp.float32)
    leave[3:8] = jnp.zeros((5, leave.shape[1]), jnp.float32)

    def leave_copy(d):
        return pltpu.make_async_remote_copy(
            src_ref=leave,
            dst_ref=met.at[d],
            send_sem=leave_send.at[d],
            recv_sem=leave_recv.at[d],
            device_id=(my_row + d, my_col),
            device_id_type=MESH,
        )

    for d in range(1, n_row):

        @pl.when(my_row + d < n_row)
        def _():
            leave_copy(d).start()

    def solve(i, carry):
        at = pl.ds(pl.multiple_of(i * 8, 8), 8)
        upper, value = [], []
        for l in range(layers):
            v = vert_ref[l, at, :]
            right = moved[l, at, :]
            if l == 0:
                surface = rain_ref[at, :] * (4.0 * moist_ref[0, at, :] * moist_ref[0, at, :])
                right = right + (rain_ref[at, :] - surface)
                diag = 1.0 + v
            else:
                diag = 1.0 + v + vl * (1.0 - upper[-1])
                right = right + vl * value[-1]
            inverse = 1.0 / diag
            upper.append(v * inverse)
            value.append(right * inverse)
            vl = v
        x = value[-1]
        new_ref[layers - 1, at, :] = x
        for l in range(layers - 2, -1, -1):
            x = value[l] + upper[l] * x
            new_ref[l, at, :] = x
        return carry

    lax.fori_loop(0, rows // 8, solve, 0)

    boundary[...] = jnp.zeros_like(boundary)
    reach_lane = lax.broadcasted_iota(jnp.int32, (128, 128), 0).astype(jnp.float32)
    for d in range(n_row - 1, 0, -1):

        @pl.when(my_row >= d)
        def _():
            leave_copy(d).wait_recv()
            block = met[d]
            goal = jnp.where(reach_lane == block[2:3], 1.0, 0.0).astype(jnp.bfloat16)
            flow = jnp.broadcast_to(block[0:1] * boundary[0:1] + block[1:2], (16, 128))
            first, left = bf16_split(flow)
            row16 = lax.broadcasted_iota(jnp.int32, (16, 128), 0)
            remain = flow - first.astype(jnp.float32)
            second = remain.astype(jnp.bfloat16)
            third = (remain - second.astype(jnp.float32))
            pieces = jnp.where(
                row16 == 0,
                first.astype(jnp.float32),
                jnp.where(row16 == 1, second.astype(jnp.float32), jnp.where(row16 == 2, third, 0.0)),
            ).astype(jnp.bfloat16)
            got = lax.dot_general(pieces, goal, NT, preferred_element_type=jnp.float32)
            boundary[0:1] = got[0:1] + got[1:2] + got[2:3]

    enter = boundary[0:1]
    flows = [gains[i] * enter + offsets[i] for i in range(segments)]
    flow_ref[...] = jnp.concatenate(flows, 0)
    inflow_ref[...] = jnp.concatenate([enter] + flows[:-1], 0) + lateral_flow

    @pl.when(has_up)
    def _():
        row_copy(0, True).wait_send()
        row_copy(1, True).wait_send()

    @pl.when(has_down)
    def _():
        row_copy(0, False).wait_send()
        row_copy(1, False).wait_send()

    @pl.when(has_left)
    def _():
        col_copy(True).wait_send()

    @pl.when(has_right)
    def _():
        col_copy(False).wait_send()

    for d in range(1, n_row):

        @pl.when(my_row + d < n_row)
        def _():
            leave_copy(d).wait_send()


def whole_step(moisture, lateral_cond, vertical_cond, rain, sent, reach, travel, out_b, in_b, outlet):
    layers, rows, cols = moisture.shape
    devices = sent.shape[0]
    n_row = lax.axis_size("row")
    height, width = rows + 8, cols + 128
    f32 = jnp.float32
    vmem = pl.BlockSpec(memory_space=pltpu.VMEM)
    dma = pltpu.SemaphoreType.DMA
    return pl.pallas_call(
        step_kernel,
        in_specs=[vmem] * 10,
        out_specs=[vmem] * 3,
        out_shape=[
            jax.ShapeDtypeStruct(moisture.shape, f32),
            jax.ShapeDtypeStruct(travel.shape, f32),
            jax.ShapeDtypeStruct(travel.shape, f32),
        ],
        scratch_shapes=[
            pltpu.VMEM((layers, height, width), f32),
            pltpu.VMEM((layers, height, width), f32),
            pltpu.VMEM((layers, rows, cols), f32),
            pltpu.VMEM((2, layers, 8, cols), f32),
            pltpu.VMEM((2, layers, 8, cols), f32),
            pltpu.VMEM((height, 128), f32),
            pltpu.VMEM((height, 128), f32),
            pltpu.VMEM((height, 128), f32),
            pltpu.VMEM((height, 128), f32),
            pltpu.VMEM((devices, 8, 128), f32),
            pltpu.VMEM((8, 128), f32),
            pltpu.VMEM((n_row, 8, 128), f32),
            pltpu.VMEM((8, 128), f32),
            dma((devices,)),
            dma((devices,)),
            dma((4,)),
            dma((4,)),
            dma((2,)),
            dma((2,)),
            dma,
            dma((n_row,)),
            dma((n_row,)),
        ],
        compiler_params=pltpu.CompilerParams(
            collective_id=0, has_side_effects=True, vmem_limit_bytes=40 * 1024 * 1024
        ),
        name="whole_step",
    )(moisture, lateral_cond, vertical_cond, rain, sent, reach, travel, out_b, in_b, outlet)


def shards(
    moisture,
    lateral_cond,
    vertical_cond,
    rain,
    remap_cell,
    remap_reach,
    travel_time,
    outflow_before,
    inflow_before,
    outlet_lane,
):
    sent = look_up(moisture, vertical_cond, rain, remap_cell)
    reach = remap_reach.reshape(sent.shape)
    return tuple(
        whole_step(
            moisture, lateral_cond, vertical_cond, rain, sent, reach,
            travel_time, outflow_before, inflow_before, outlet_lane,
        )
    )


def solution(mesh):
    in_specs = (
        P(None, "row", "col"),
        P(None, "row", "col"),
        P(None, "row", "col"),
        P("row", "col"),
        P(("row", "col"), None, None),
        P(None, ("row", "col"), None),
        P("row", "col"),
        P("row", "col"),
        P("row", "col"),
        P("row", "col"),
    )
    out_specs = (P(None, "row", "col"), P("row", "col"), P("row", "col"))
    return jax.shard_map(shards, mesh=mesh, in_specs=in_specs, out_specs=out_specs, check_vma=False)
```

```python
import functools
import math

import jax
import jax.numpy as jnp
from jax import lax
from jax.experimental import pallas as pl
from jax.experimental.pallas import tpu as pltpu
from jax.sharding import PartitionSpec as P

SUB = 3
WEIGHT_X = 0.2
SIDEWAYS_FACTOR = 0.01

RUNOFF_LOW = 0.0025
RUNOFF_HIGH = 1.31
LOG_LOW = math.log(RUNOFF_LOW)
CODE_MAX = 65535.0
LOG_STEP = (math.log(RUNOFF_HIGH) - LOG_LOW) / CODE_MAX

UNROLL = 4
MESH = pl.DeviceIdType.MESH
NT = (((1,), (1,)), ((), ()))


def lookup_kernel(
    moist_ref, vert_ref, rain_ref, cell_ref, out_ref,
    fields, cells, table, stage, looked, counts_vec, counts, chunks, sem, fetch_sem,
):
    dests, per = cells.shape[0:2]
    last = moist_ref.shape[0] - 1
    parts = [moist_ref.at[0], moist_ref.at[last], vert_ref.at[last], rain_ref]
    field_fetches = [
        pltpu.make_async_copy(part, fields.at[i], fetch_sem.at[per + i])
        for i, part in enumerate(parts)
    ]
    for fetch in field_fetches:
        fetch.start()
    fetches = [
        pltpu.make_async_copy(
            cell_ref.at[0, :, j * 128 : (j + 1) * 128], cells.at[:, j, :], fetch_sem.at[j]
        )
        for j in range(per)
    ]
    for fetch in fetches:
        fetch.start()

    for fetch in field_fetches:
        fetch.wait()
    runoff = fields[3] * (4.0 * fields[0] * fields[0]) + fields[2] * fields[1]
    code = (jnp.log(runoff) - LOG_LOW) * (1.0 / LOG_STEP)
    code = jnp.clip(jnp.round(code), 0.0, CODE_MAX).astype(jnp.int32)
    rows = runoff.shape[0]
    for k in range(2):
        low = code[:, k * 128 : (k + 1) * 128]
        high = code[:, (k + 2) * 128 : (k + 3) * 128]
        table[k * rows : (k + 1) * rows, :] = low | (high << 16)

    out_ref[...] = jnp.zeros_like(out_ref)

    for fetch in fetches:
        fetch.wait()
    live = jnp.sum(jnp.where(cells[...] >= 0, 1, 0), axis=1)
    counts_vec[...] = jnp.transpose(live)[0:8, :]
    copy = pltpu.make_async_copy(counts_vec, counts, sem)
    copy.start()
    copy.wait()

    def enlist(d, total):
        for j in range(per):
            chunks[total + j] = d * per + j
        return total + counts[0, d]

    total = lax.fori_loop(0, dests, enlist, jnp.int32(0))
    for i in range(8 * UNROLL):
        chunks[total + i] = 0

    def step(g, carry):
        for u in range(UNROLL):
            for s in range(8):
                e = chunks[(g * UNROLL + u) * 8 + s]
                stage[u, s : s + 1, :] = cells[e >> 3, pl.ds(e & 7, 1), :]
        for u in range(UNROLL):
            cell = stage[u]
            lane = cell & 127
            word_row = ((cell >> 9) & 63) | ((cell >> 1) & 64)
            odd = [None, None]
            for t in range(2 * rows):
                row = jnp.broadcast_to(table[t : t + 1, :], (8, 128))
                got = jnp.take_along_axis(row, lane, axis=1, mode="promise_in_bounds")
                old = odd[t % 2]
                odd[t % 2] = got if old is None else jnp.where(word_row == t, got, old)
            word = jnp.where((word_row & 1) == 1, odd[1], odd[0])
            half = jnp.where(((cell >> 8) & 1) == 1, word >> 16, word) & 65535
            value = jnp.exp(half.astype(jnp.float32) * LOG_STEP + LOG_LOW)
            looked[u] = jnp.where(cell >= 0, value, 0.0)
        for u in range(UNROLL):
            for s in range(8):
                e = chunks[(g * UNROLL + u) * 8 + s]
                out_ref[e >> 3, pl.ds(e & 7, 1), :] = looked[u, s : s + 1, :]
        return carry

    lax.fori_loop(0, (total + (8 * UNROLL - 1)) // (8 * UNROLL), step, 0)


def look_up(moisture, vertical_cond, rain, remap_cell):
    layers, rows, cols = moisture.shape
    dests, slots = remap_cell.shape[1:]
    return pl.pallas_call(
        lookup_kernel,
        in_specs=[pl.BlockSpec(memory_space=pltpu.HBM)] * 4,
        out_specs=pl.BlockSpec(memory_space=pltpu.VMEM),
        out_shape=jax.ShapeDtypeStruct((dests, slots // 128, 128), jnp.float32),
        scratch_shapes=[
            pltpu.VMEM((4, rows, cols), jnp.float32),
            pltpu.VMEM((dests, slots // 128, 128), jnp.int32),
            pltpu.VMEM((2 * rows, 128), jnp.int32),
            pltpu.VMEM((UNROLL, 8, 128), jnp.int32),
            pltpu.VMEM((UNROLL, 8, 128), jnp.float32),
            pltpu.VMEM((8, dests), jnp.int32),
            pltpu.SMEM((8, dests), jnp.int32),
            pltpu.SMEM((dests * (slots // 128) + 8 * UNROLL + 8,), jnp.int32),
            pltpu.SemaphoreType.DMA,
            pltpu.SemaphoreType.DMA((slots // 128 + 4,)),
        ],
        compiler_params=pltpu.CompilerParams(vmem_limit_bytes=53 * 1024 * 1024),
        name="look_up",
    )(moisture, vertical_cond, rain, remap_cell)


GROUP = 8
HALF_BINS = 64


def step_kernel(
    moist_ref, cond_ref, sent_ref, reach_ref,
    travel_ref, out_before_ref, in_before_ref, outlet_ref,
    moved_ref, flow_ref, inflow_ref,
    edge_rows, edge_cols, pack_up, pack_down, below, above, pack_left, pack_right, from_right, from_left,
    arrived, rows_of, leave, met, boundary,
    send_sem, recv_sem, row_send, row_recv, col_send, col_recv, own_sem, leave_send, leave_recv,
):
    n_row, n_col = lax.axis_size("row"), lax.axis_size("col")
    devices = n_row * n_col
    my_row, my_col = lax.axis_index("row"), lax.axis_index("col")
    me = my_row * n_col + my_col
    layers, rows, cols = moist_ref.shape
    height, width = rows + 8, cols + 128
    fields = (moist_ref, cond_ref)

    barrier = pltpu.get_barrier_semaphore()

    def greet(k, carry):
        other = lax.rem(me + k, devices)
        pl.semaphore_signal(
            barrier, inc=1, device_id=(other // n_col, lax.rem(other, n_col)), device_id_type=MESH
        )
        return carry

    lax.fori_loop(1, devices, greet, 0)

    travel = travel_ref[...]
    denom = 1.0 / (1.0 + 2.0 * travel * (1.0 - WEIGHT_X))
    gain = (1.0 - 2.0 * travel * WEIGHT_X) * denom
    rest = (1.0 + 2.0 * travel * WEIGHT_X) * denom * in_before_ref[...]
    rest += (2.0 * travel * (1.0 - WEIGHT_X) - 1.0) * denom * out_before_ref[...]

    has_up, has_down = my_row > 0, my_row < n_row - 1
    has_left, has_right = my_col > 0, my_col < n_col - 1

    sub = lax.broadcasted_iota(jnp.int32, (layers, 8, cols), 1)
    pack_up[...] = jnp.where(
        sub < SUB, moist_ref[:, 0:8, :], pltpu.roll(cond_ref[:, 0:8, :], 8 - SUB, 1)
    )
    pack_down[...] = jnp.where(
        sub >= 8 - SUB,
        moist_ref[:, rows - 8 : rows, :],
        pltpu.roll(cond_ref[:, rows - 8 : rows, :], SUB, 1),
    )

    def row_copy(up):
        return pltpu.make_async_remote_copy(
            src_ref=pack_up if up else pack_down,
            dst_ref=below if up else above,
            send_sem=row_send.at[0 if up else 1],
            recv_sem=row_recv.at[0 if up else 1],
            device_id=(my_row - 1 if up else my_row + 1, my_col),
            device_id_type=MESH,
        )

    pl.semaphore_wait(barrier, devices - 1)

    def list_copy(k):
        other = lax.rem(me + k, devices)
        return pltpu.make_async_remote_copy(
            src_ref=sent_ref.at[other],
            dst_ref=arrived.at[k],
            send_sem=send_sem.at[k],
            recv_sem=recv_sem.at[k],
            device_id=(other // n_col, lax.rem(other, n_col)),
            device_id_type=MESH,
        )

    def send_list(k, carry):
        list_copy(k).start()
        return carry

    lax.fori_loop(1, devices, send_list, 0)
    @pl.when(has_up)
    def _():
        row_copy(True).start()

    @pl.when(has_down)
    def _():
        row_copy(False).start()

    own = pltpu.make_async_copy(sent_ref.at[me], arrived.at[0], own_sem)
    own.start()

    own.wait()
    base = lax.broadcasted_iota(jnp.int32, (16, 1024), 0).astype(jnp.float32).astype(jnp.bfloat16)
    zero = jnp.zeros((16, 1024), jnp.bfloat16)
    one = jnp.ones((16, 1024), jnp.bfloat16)

    def spread(u, i):
        return jnp.concatenate(
            [
                jnp.broadcast_to(rows_of[u, i, j : j + 1, :], (16, 128)).astype(jnp.bfloat16)
                for j in range(8)
            ],
            1,
        )

    def add_up(g, acc):
        for u in range(GROUP):
            k = g * GROUP + u

            @pl.when(k > 0)
            def _():
                list_copy(k).wait()

        for u in range(GROUP):
            k = g * GROUP + u
            q = reach_ref[lax.rem(me - k + devices, devices)]
            value = arrived[k]
            head = value.astype(jnp.bfloat16).astype(jnp.float32)
            rows_of[u, 0] = ((q >> 7) + 16 * ((q >> 6) & 1)).astype(jnp.float32)
            rows_of[u, 1] = (q & 63).astype(jnp.float32)
            rows_of[u, 2] = head
            rows_of[u, 3] = value - head
        for u in range(GROUP):
            a, b, head, tail = [spread(u, i) for i in range(4)]
            hits = [base + jnp.bfloat16(16 * t) == a for t in range(2)]
            values = jnp.concatenate(
                [jnp.where(h, head, zero) for h in hits] + [jnp.where(h, tail, zero) for h in hits], 0
            )
            places = jnp.concatenate(
                [jnp.where(base + jnp.bfloat16(16 * t) == b, one, zero) for t in range(4)], 0
            )
            acc = acc + lax.dot_general(values, places, NT, preferred_element_type=jnp.float32)
        return acc

    turns = devices // GROUP
    bins = lax.fori_loop(0, turns // 2, add_up, jnp.zeros((64, HALF_BINS), jnp.float32))

    edge_rows[...] = jnp.zeros_like(edge_rows)

    @pl.when(has_down)
    def _():
        row_copy(True).wait_recv()
        edge_rows[0] = jnp.where(sub < SUB, below[...], 0.0)
        edge_rows[1] = jnp.where(sub < SUB, pltpu.roll(below[...], SUB, 1), 0.0)

    @pl.when(has_up)
    def _():
        row_copy(False).wait_recv()
        edge_rows[0] = jnp.where(sub >= 8 - SUB, above[...], edge_rows[0])
        edge_rows[1] = jnp.where(sub >= 8 - SUB, pltpu.roll(above[...], 8 - SUB, 1), edge_rows[1])

    def tall(f, l, lanes):
        return jnp.concatenate([fields[f][l, :, lanes], edge_rows[f, l, :, lanes]], 0)

    lane = lax.broadcasted_iota(jnp.int32, (height, 128), 1)
    left_pack = jnp.zeros((height, 128), jnp.float32)
    right_pack = jnp.zeros((height, 128), jnp.float32)
    for p in range(2 * layers):
        here = (lane >= SUB * p) & (lane < SUB * (p + 1))
        first = tall(p // layers, p % layers, slice(0, 128))
        last = tall(p // layers, p % layers, slice(cols - 128, cols))
        left_pack = jnp.where(here, pltpu.roll(first, SUB * p, 1) if p else first, left_pack)
        right_pack = jnp.where(here, pltpu.roll(last, SUB * p + SUB, 1), right_pack)
    pack_left[...] = left_pack
    pack_right[...] = right_pack

    def col_copy(left):
        return pltpu.make_async_remote_copy(
            src_ref=pack_left if left else pack_right,
            dst_ref=from_right if left else from_left,
            send_sem=col_send.at[0 if left else 1],
            recv_sem=col_recv.at[0 if left else 1],
            device_id=(my_row, my_col - 1 if left else my_col + 1),
            device_id_type=MESH,
        )

    @pl.when(has_left)
    def _():
        col_copy(True).start()

    @pl.when(has_right)
    def _():
        col_copy(False).start()

    bins = lax.fori_loop(turns // 2, turns, add_up, bins)
    bins = SIDEWAYS_FACTOR * (bins[0:32] + bins[32:64])
    lateral_flow = jnp.concatenate([bins[0:16], bins[16:32]], 1)

    segments = lateral_flow.shape[0]
    offset_term = gain * lateral_flow + rest
    gains, offsets = [gain[0:1]], [offset_term[0:1]]
    for i in range(1, segments):
        g = gain[i : i + 1]
        gains.append(g * gains[-1])
        offsets.append(g * offsets[-1] + offset_term[i : i + 1])

    leave[0:1] = gains[-1]
    leave[1:2] = offsets[-1]
    leave[2:3] = outlet_ref[...].astype(jnp.float32)
    leave[3:8] = jnp.zeros((5, leave.shape[1]), jnp.float32)

    def leave_copy(d):
        return pltpu.make_async_remote_copy(
            src_ref=leave,
            dst_ref=met.at[d],
            send_sem=leave_send.at[d],
            recv_sem=leave_recv.at[d],
            device_id=(my_row + d, my_col),
            device_id_type=MESH,
        )

    for d in range(1, n_row):

        @pl.when(my_row + d < n_row)
        def _():
            leave_copy(d).start()

    edge_cols[...] = jnp.zeros_like(edge_cols)

    @pl.when(has_right)
    def _():
        col_copy(True).wait_recv()
        packed = from_right[...]
        for p in range(2 * layers):
            part = pltpu.roll(packed, 128 - SUB * p, 1) if p else packed
            edge_cols[p // layers, p % layers] = jnp.where(lane < SUB, part, 0.0)

    @pl.when(has_left)
    def _():
        col_copy(False).wait_recv()
        packed = from_left[...]
        for p in range(2 * layers):
            part = pltpu.roll(packed, 128 - SUB - SUB * p, 1)
            edge_cols[p // layers, p % layers] = jnp.where(
                lane >= 128 - SUB, part, edge_cols[p // layers, p % layers]
            )

    def lateral(l, carry):
        m, c = [
            jnp.concatenate([tall(f, l, slice(0, cols)), edge_cols[f, l]], 1) for f in range(2)
        ]
        down, right = pltpu.roll(c, height - 1, 0), pltpu.roll(c, width - 1, 1)
        face_down = 2.0 * c * down / jnp.maximum(c + down, 1e-30)
        face_right = 2.0 * c * right / jnp.maximum(c + right, 1e-30)
        for _ in range(SUB):
            flux_down = face_down * (pltpu.roll(m, height - 1, 0) - m)
            flux_right = face_right * (pltpu.roll(m, width - 1, 1) - m)
            m = m + (
                (flux_down - pltpu.roll(flux_down, 1, 0))
                + (flux_right - pltpu.roll(flux_right, 1, 1))
            )
        moved_ref[l] = m[0:rows, 0:cols]
        return carry

    lax.fori_loop(0, layers, lateral, 0)

    boundary[...] = jnp.zeros_like(boundary)
    reach_lane = lax.broadcasted_iota(jnp.int32, (128, 128), 0).astype(jnp.float32)
    row16 = lax.broadcasted_iota(jnp.int32, (16, 128), 0)
    for d in range(n_row - 1, 0, -1):

        @pl.when(my_row >= d)
        def _():
            leave_copy(d).wait_recv()
            block = met[d]
            goal = jnp.where(reach_lane == block[2:3], 1.0, 0.0).astype(jnp.bfloat16)
            flow = jnp.broadcast_to(block[0:1] * boundary[0:1] + block[1:2], (16, 128))
            first = flow.astype(jnp.bfloat16).astype(jnp.float32)
            second = (flow - first).astype(jnp.bfloat16).astype(jnp.float32)
            third = flow - first - second
            pieces = jnp.where(
                row16 == 0, first, jnp.where(row16 == 1, second, jnp.where(row16 == 2, third, 0.0))
            ).astype(jnp.bfloat16)
            got = lax.dot_general(pieces, goal, NT, preferred_element_type=jnp.float32)
            boundary[0:1] = got[0:1] + got[1:2] + got[2:3]

    enter = boundary[0:1]
    flows = [gains[i] * enter + offsets[i] for i in range(segments)]
    flow_ref[...] = jnp.concatenate(flows, 0)
    inflow_ref[...] = jnp.concatenate([enter] + flows[:-1], 0) + lateral_flow

    @pl.when(has_up)
    def _():
        row_copy(True).wait_send()

    @pl.when(has_down)
    def _():
        row_copy(False).wait_send()

    @pl.when(has_left)
    def _():
        col_copy(True).wait_send()

    @pl.when(has_right)
    def _():
        col_copy(False).wait_send()

    for d in range(1, n_row):

        @pl.when(my_row + d < n_row)
        def _():
            leave_copy(d).wait_send()


def exchange_step(moisture, lateral_cond, sent, reach, travel, out_b, in_b, outlet):
    layers, rows, cols = moisture.shape
    devices = sent.shape[0]
    n_row = lax.axis_size("row")
    height = rows + 8
    f32 = jnp.float32
    vmem = pl.BlockSpec(memory_space=pltpu.VMEM)
    dma = pltpu.SemaphoreType.DMA
    return pl.pallas_call(
        step_kernel,
        in_specs=[vmem] * 8,
        out_specs=[vmem] * 3,
        out_shape=[
            jax.ShapeDtypeStruct(moisture.shape, f32),
            jax.ShapeDtypeStruct(travel.shape, f32),
            jax.ShapeDtypeStruct(travel.shape, f32),
        ],
        scratch_shapes=[
            pltpu.VMEM((2, layers, 8, cols), f32),
            pltpu.VMEM((2, layers, height, 128), f32),
            pltpu.VMEM((layers, 8, cols), f32),
            pltpu.VMEM((layers, 8, cols), f32),
            pltpu.VMEM((layers, 8, cols), f32),
            pltpu.VMEM((layers, 8, cols), f32),
            pltpu.VMEM((height, 128), f32),
            pltpu.VMEM((height, 128), f32),
            pltpu.VMEM((height, 128), f32),
            pltpu.VMEM((height, 128), f32),
            pltpu.VMEM((devices, 8, 128), f32),
            pltpu.VMEM((GROUP, 4, 8, 128), f32),
            pltpu.VMEM((8, 128), f32),
            pltpu.VMEM((n_row, 8, 128), f32),
            pltpu.VMEM((8, 128), f32),
            dma((devices,)),
            dma((devices,)),
            dma((2,)),
            dma((2,)),
            dma((2,)),
            dma((2,)),
            dma,
            dma((n_row,)),
            dma((n_row,)),
        ],
        compiler_params=pltpu.CompilerParams(
            collective_id=0, has_side_effects=True, vmem_limit_bytes=24 * 1024 * 1024
        ),
        name="exchange_step",
    )(moisture, lateral_cond, sent, reach, travel, out_b, in_b, outlet)


def finish_kernel(
    moved_ref, vert_ref, rain_ref, moist_ref, flow_in_ref, inflow_in_ref,
    new_ref, flow_ref, inflow_ref,
    solved, new_sem, flow_sem,
):
    layers, rows, _ = moved_ref.shape
    steps = rows // 8
    flow_copies = [
        pltpu.make_async_copy(flow_in_ref, flow_ref, flow_sem.at[0]),
        pltpu.make_async_copy(inflow_in_ref, inflow_ref, flow_sem.at[1]),
    ]
    for copy in flow_copies:
        copy.start()

    def new_copy(i):
        at = pl.ds(pl.multiple_of(i * 8, 8), 8)
        return pltpu.make_async_copy(solved.at[:, at, :], new_ref.at[:, at, :], new_sem.at[i])

    def solve(i, carry):
        at = pl.ds(pl.multiple_of(i * 8, 8), 8)
        upper, value = [], []
        for l in range(layers):
            v = vert_ref[l, at, :]
            right = moved_ref[l, at, :]
            if l == 0:
                wet = moist_ref[0, at, :]
                right = right + (rain_ref[at, :] - rain_ref[at, :] * (4.0 * wet * wet))
                diag = 1.0 + v
            else:
                diag = 1.0 + v + above * (1.0 - upper[-1])
                right = right + above * value[-1]
            inverse = 1.0 / diag
            upper.append(v * inverse)
            value.append(right * inverse)
            above = v
        x = value[-1]
        solved[layers - 1, at, :] = x
        for l in range(layers - 2, -1, -1):
            x = value[l] + upper[l] * x
            solved[l, at, :] = x
        new_copy(i).start()
        return carry

    lax.fori_loop(0, steps, solve, 0)
    for copy in flow_copies:
        copy.wait()
    for i in range(steps):
        new_copy(i).wait()


def finish(moved, vertical_cond, rain, moisture, flow, inflow):
    vmem = pl.BlockSpec(memory_space=pltpu.VMEM)
    out = pl.BlockSpec(memory_space=pl.ANY)
    return pl.pallas_call(
        finish_kernel,
        in_specs=[vmem] * 6,
        out_specs=[out] * 3,
        out_shape=[
            jax.ShapeDtypeStruct(moved.shape, jnp.float32),
            jax.ShapeDtypeStruct(flow.shape, jnp.float32),
            jax.ShapeDtypeStruct(flow.shape, jnp.float32),
        ],
        scratch_shapes=[
            pltpu.VMEM(moved.shape, jnp.float32),
            pltpu.SemaphoreType.DMA((moved.shape[1] // 8,)),
            pltpu.SemaphoreType.DMA((2,)),
        ],
        compiler_params=pltpu.CompilerParams(vmem_limit_bytes=16 * 1024 * 1024),
        name="finish",
    )(moved, vertical_cond, rain, moisture, flow, inflow)


def shards(
    moisture,
    lateral_cond,
    vertical_cond,
    rain,
    remap_cell,
    remap_reach,
    travel_time,
    outflow_before,
    inflow_before,
    outlet_lane,
):
    sent = look_up(moisture, vertical_cond, rain, remap_cell)
    reach = remap_reach.reshape(sent.shape)
    moved, flow, inflow = exchange_step(
        moisture, lateral_cond, sent, reach, travel_time, outflow_before, inflow_before, outlet_lane
    )
    return tuple(finish(moved, vertical_cond, rain, moisture, flow, inflow))


def solution(mesh):
    in_specs = (
        P(None, "row", "col"),
        P(None, "row", "col"),
        P(None, "row", "col"),
        P("row", "col"),
        P(("row", "col"), None, None),
        P(None, ("row", "col"), None),
        P("row", "col"),
        P("row", "col"),
        P("row", "col"),
        P("row", "col"),
    )
    out_specs = (P(None, "row", "col"), P("row", "col"), P("row", "col"))
    return jax.shard_map(shards, mesh=mesh, in_specs=in_specs, out_specs=out_specs, check_vma=False)
```

```python
import functools
import math

import jax
import jax.numpy as jnp
from jax import lax
from jax.experimental import pallas as pl
from jax.experimental.pallas import tpu as pltpu
from jax.sharding import PartitionSpec as P

SUB = 3
WEIGHT_X = 0.2
SIDEWAYS_FACTOR = 0.01

RUNOFF_LOW = 0.0025
RUNOFF_HIGH = 1.31
LOG_LOW = math.log(RUNOFF_LOW)
CODE_MAX = 65535.0
LOG_STEP = (math.log(RUNOFF_HIGH) - LOG_LOW) / CODE_MAX

UNROLL = 8
MESH = pl.DeviceIdType.MESH
NT = (((1,), (1,)), ((), ()))


def lookup_kernel(
    moist_ref, vert_ref, rain_ref, cell_ref, out_ref,
    fields, cells, table, stage, looked, counts_vec, counts, chunks, sem, fetch_sem,
):
    dests, per = cells.shape[0:2]
    last = moist_ref.shape[0] - 1
    parts = [moist_ref.at[0], moist_ref.at[last], vert_ref.at[last], rain_ref]
    field_fetches = [
        pltpu.make_async_copy(part, fields.at[i], fetch_sem.at[per + i])
        for i, part in enumerate(parts)
    ]
    for fetch in field_fetches:
        fetch.start()
    fetches = [
        pltpu.make_async_copy(
            cell_ref.at[0, :, j * 128 : (j + 1) * 128], cells.at[:, j, :], fetch_sem.at[j]
        )
        for j in range(per)
    ]
    for fetch in fetches:
        fetch.start()

    for fetch in field_fetches:
        fetch.wait()
    runoff = fields[3] * (4.0 * fields[0] * fields[0]) + fields[2] * fields[1]
    code = (jnp.log(runoff) - LOG_LOW) * (1.0 / LOG_STEP)
    code = jnp.clip(jnp.round(code), 0.0, CODE_MAX).astype(jnp.int32)
    rows = runoff.shape[0]
    for k in range(2):
        low = code[:, k * 128 : (k + 1) * 128]
        high = code[:, (k + 2) * 128 : (k + 3) * 128]
        table[k * rows : (k + 1) * rows, :] = low | (high << 16)

    out_ref[...] = jnp.zeros_like(out_ref)

    for fetch in fetches:
        fetch.wait()
    live = jnp.sum(jnp.where(cells[...] >= 0, 1, 0), axis=1)
    counts_vec[...] = jnp.transpose(live)[0:8, :]
    copy = pltpu.make_async_copy(counts_vec, counts, sem)
    copy.start()
    copy.wait()

    def enlist(d, total):
        for j in range(per):
            chunks[total + j] = d * per + j
        return total + counts[0, d]

    total = lax.fori_loop(0, dests, enlist, jnp.int32(0))
    for i in range(8 * UNROLL):
        chunks[total + i] = 0

    def step(g, carry):
        for u in range(UNROLL):
            for s in range(8):
                e = chunks[(g * UNROLL + u) * 8 + s]
                stage[u, s : s + 1, :] = cells[e >> 3, pl.ds(e & 7, 1), :]
        for u in range(UNROLL):
            cell = stage[u]
            lane = cell & 127
            word_row = ((cell >> 9) & 63) | ((cell >> 1) & 64)
            odd = [None, None]
            for t in range(2 * rows):
                row = jnp.broadcast_to(table[t : t + 1, :], (8, 128))
                got = jnp.take_along_axis(row, lane, axis=1, mode="promise_in_bounds")
                old = odd[t % 2]
                odd[t % 2] = got if old is None else jnp.where(word_row == t, got, old)
            word = jnp.where((word_row & 1) == 1, odd[1], odd[0])
            half = jnp.where(((cell >> 8) & 1) == 1, word >> 16, word) & 65535
            value = jnp.exp(half.astype(jnp.float32) * LOG_STEP + LOG_LOW)
            looked[u] = jnp.where(cell >= 0, value, 0.0)
        for u in range(UNROLL):
            for s in range(8):
                e = chunks[(g * UNROLL + u) * 8 + s]
                out_ref[e >> 3, pl.ds(e & 7, 1), :] = looked[u, s : s + 1, :]
        return carry

    lax.fori_loop(0, (total + (8 * UNROLL - 1)) // (8 * UNROLL), step, 0)


def look_up(moisture, vertical_cond, rain, remap_cell):
    layers, rows, cols = moisture.shape
    dests, slots = remap_cell.shape[1:]
    return pl.pallas_call(
        lookup_kernel,
        in_specs=[pl.BlockSpec(memory_space=pltpu.HBM)] * 4,
        out_specs=pl.BlockSpec(memory_space=pltpu.VMEM),
        out_shape=jax.ShapeDtypeStruct((dests, slots // 128, 128), jnp.float32),
        scratch_shapes=[
            pltpu.VMEM((4, rows, cols), jnp.float32),
            pltpu.VMEM((dests, slots // 128, 128), jnp.int32),
            pltpu.VMEM((2 * rows, 128), jnp.int32),
            pltpu.VMEM((UNROLL, 8, 128), jnp.int32),
            pltpu.VMEM((UNROLL, 8, 128), jnp.float32),
            pltpu.VMEM((8, dests), jnp.int32),
            pltpu.SMEM((8, dests), jnp.int32),
            pltpu.SMEM((dests * (slots // 128) + 8 * UNROLL + 8,), jnp.int32),
            pltpu.SemaphoreType.DMA,
            pltpu.SemaphoreType.DMA((slots // 128 + 4,)),
        ],
        compiler_params=pltpu.CompilerParams(vmem_limit_bytes=53 * 1024 * 1024),
        name="look_up",
    )(moisture, vertical_cond, rain, remap_cell)


HALF_BINS = 64


def step_kernel(
    moist_ref, cond_ref, sent_ref, reach_ref,
    travel_ref, out_before_ref, in_before_ref, outlet_ref,
    moved_ref, flow_ref, inflow_ref,
    edge_rows, edge_cols, pack_up, pack_down, below, above, pack_left, pack_right, from_right, from_left,
    arrived, faces, leave, met, boundary,
    send_sem, recv_sem, row_send, row_recv, col_send, col_recv, own_sem, leave_send, leave_recv,
):
    n_row, n_col = lax.axis_size("row"), lax.axis_size("col")
    devices = n_row * n_col
    my_row, my_col = lax.axis_index("row"), lax.axis_index("col")
    me = my_row * n_col + my_col
    layers, rows, cols = moist_ref.shape
    height, width = rows + 8, cols + 128
    fields = (moist_ref, cond_ref)

    barrier = pltpu.get_barrier_semaphore()

    def wrap(x, size):
        return jnp.where(x >= size, x - size, x)

    ahead = [wrap(my_col + dc, n_col) for dc in range(n_col)]
    behind = [wrap(my_col + n_col - dc, n_col) for dc in range(n_col)]

    def greet(dr, first):
        row = wrap(my_row + dr, n_row)
        for dc in range(first, n_col):
            pl.semaphore_signal(
                barrier, inc=1, device_id=(row, ahead[dc]), device_id_type=MESH
            )

    greet(0, 1)

    @pl.loop(1, n_row)
    def _(dr):
        greet(dr, 0)

    travel = travel_ref[...]
    denom = 1.0 / (1.0 + 2.0 * travel * (1.0 - WEIGHT_X))
    gain = (1.0 - 2.0 * travel * WEIGHT_X) * denom
    rest = (1.0 + 2.0 * travel * WEIGHT_X) * denom * in_before_ref[...]
    rest += (2.0 * travel * (1.0 - WEIGHT_X) - 1.0) * denom * out_before_ref[...]

    has_up, has_down = my_row > 0, my_row < n_row - 1
    has_left, has_right = my_col > 0, my_col < n_col - 1

    sub = lax.broadcasted_iota(jnp.int32, (layers, 8, cols), 1)
    pack_up[...] = jnp.where(
        sub < SUB, moist_ref[:, 0:8, :], pltpu.roll(cond_ref[:, 0:8, :], 8 - SUB, 1)
    )
    pack_down[...] = jnp.where(
        sub >= 8 - SUB,
        moist_ref[:, rows - 8 : rows, :],
        pltpu.roll(cond_ref[:, rows - 8 : rows, :], SUB, 1),
    )

    def row_copy(up):
        return pltpu.make_async_remote_copy(
            src_ref=pack_up if up else pack_down,
            dst_ref=below if up else above,
            send_sem=row_send.at[0 if up else 1],
            recv_sem=row_recv.at[0 if up else 1],
            device_id=(my_row - 1 if up else my_row + 1, my_col),
            device_id_type=MESH,
        )

    pl.semaphore_wait(barrier, devices - 1)

    def send_lists(dr, first):
        row = wrap(my_row + dr, n_row)
        for dc in range(first, n_col):
            pltpu.make_async_remote_copy(
                src_ref=sent_ref.at[row * n_col + ahead[dc]],
                dst_ref=arrived.at[dr * n_col + dc],
                send_sem=send_sem,
                recv_sem=recv_sem.at[dr],
                device_id=(row, ahead[dc]),
                device_id_type=MESH,
            ).start()

    send_lists(0, 1)

    @pl.loop(1, n_row)
    def _(dr):
        send_lists(dr, 0)

    def lists_wait(sem, first, count):
        place = arrived.at[pl.ds(first, count)]
        pltpu.make_async_copy(place, place, sem).wait()

    @pl.when(has_up)
    def _():
        row_copy(True).start()

    @pl.when(has_down)
    def _():
        row_copy(False).start()

    own = pltpu.make_async_copy(sent_ref.at[me], arrived.at[0], own_sem)
    own.start()

    def face(c, axis):
        size = c.shape[axis]
        near = pltpu.roll(c, size - 1, axis)
        return 2.0 * c * near / jnp.maximum(c + near, 1e-30)

    def inner_faces(l, carry):
        c = cond_ref[l]
        faces[0, l] = face(c, 0)
        faces[1, l] = face(c, 1)
        return carry

    lax.fori_loop(0, layers, inner_faces, 0)

    own.wait()
    base = lax.broadcasted_iota(jnp.int32, (16, 1024), 0).astype(jnp.float32).astype(jnp.bfloat16)
    zero = jnp.zeros((16, 1024), jnp.bfloat16)
    one = jnp.ones((16, 1024), jnp.bfloat16)

    def spread(x):
        return jnp.concatenate(
            [jnp.broadcast_to(x[j : j + 1, :], (16, 128)).astype(jnp.bfloat16) for j in range(8)], 1
        )

    def add_up(dr, acc):
        row = wrap(my_row + n_row - dr, n_row)
        for dc in range(n_col):
            k = dr * n_col + dc
            q = reach_ref[row * n_col + behind[dc]]
            value = arrived[k]
            first = value.astype(jnp.bfloat16).astype(jnp.float32)
            head, tail = spread(first), spread(value - first)
            a = spread(((q >> 7) + 16 * ((q >> 6) & 1)).astype(jnp.float32))
            b = spread((q & 63).astype(jnp.float32))
            hits = [base + jnp.bfloat16(16 * t) == a for t in range(2)]
            values = jnp.concatenate(
                [jnp.where(h, head, zero) for h in hits] + [jnp.where(h, tail, zero) for h in hits], 0
            )
            places = jnp.concatenate(
                [jnp.where(base + jnp.bfloat16(16 * t) == b, one, zero) for t in range(4)], 0
            )
            acc = acc + lax.dot_general(values, places, NT, preferred_element_type=jnp.float32)
        return acc

    def wait_and_add(dr, acc):
        lists_wait(recv_sem.at[dr], dr * n_col, n_col)
        return add_up(dr, acc)

    lists_wait(recv_sem.at[0], 1, n_col - 1)
    bins = add_up(0, jnp.zeros((64, HALF_BINS), jnp.float32))
    bins = lax.fori_loop(1, n_row // 2, wait_and_add, bins)

    edge_rows[...] = jnp.zeros_like(edge_rows)

    @pl.when(has_down)
    def _():
        row_copy(True).wait_recv()
        edge_rows[0] = jnp.where(sub < SUB, below[...], 0.0)
        edge_rows[1] = jnp.where(sub < SUB, pltpu.roll(below[...], SUB, 1), 0.0)

    @pl.when(has_up)
    def _():
        row_copy(False).wait_recv()
        edge_rows[0] = jnp.where(sub >= 8 - SUB, above[...], edge_rows[0])
        edge_rows[1] = jnp.where(sub >= 8 - SUB, pltpu.roll(above[...], 8 - SUB, 1), edge_rows[1])

    def tall(f, l, lanes):
        return jnp.concatenate([fields[f][l, :, lanes], edge_rows[f, l, :, lanes]], 0)

    lane = lax.broadcasted_iota(jnp.int32, (height, 128), 1)
    left_pack = jnp.zeros((height, 128), jnp.float32)
    right_pack = jnp.zeros((height, 128), jnp.float32)
    for p in range(2 * layers):
        here = (lane >= SUB * p) & (lane < SUB * (p + 1))
        first = tall(p // layers, p % layers, slice(0, 128))
        last = tall(p // layers, p % layers, slice(cols - 128, cols))
        left_pack = jnp.where(here, pltpu.roll(first, SUB * p, 1) if p else first, left_pack)
        right_pack = jnp.where(here, pltpu.roll(last, SUB * p + SUB, 1), right_pack)
    pack_left[...] = left_pack
    pack_right[...] = right_pack

    def col_copy(left):
        return pltpu.make_async_remote_copy(
            src_ref=pack_left if left else pack_right,
            dst_ref=from_right if left else from_left,
            send_sem=col_send.at[0 if left else 1],
            recv_sem=col_recv.at[0 if left else 1],
            device_id=(my_row, my_col - 1 if left else my_col + 1),
            device_id_type=MESH,
        )

    @pl.when(has_left)
    def _():
        col_copy(True).start()

    @pl.when(has_right)
    def _():
        col_copy(False).start()

    bins = lax.fori_loop(n_row // 2, n_row, wait_and_add, bins)
    bins = SIDEWAYS_FACTOR * (bins[0:32] + bins[32:64])
    lateral_flow = jnp.concatenate([bins[0:16], bins[16:32]], 1)

    segments = lateral_flow.shape[0]
    offset_term = gain * lateral_flow + rest
    gains, offsets = [gain[0:1]], [offset_term[0:1]]
    for i in range(1, segments):
        g = gain[i : i + 1]
        gains.append(g * gains[-1])
        offsets.append(g * offsets[-1] + offset_term[i : i + 1])

    leave[0:1] = gains[-1]
    leave[1:2] = offsets[-1]
    leave[2:3] = outlet_ref[...].astype(jnp.float32)
    leave[3:8] = jnp.zeros((5, leave.shape[1]), jnp.float32)

    def leave_copy(d):
        return pltpu.make_async_remote_copy(
            src_ref=leave,
            dst_ref=met.at[d],
            send_sem=leave_send.at[d],
            recv_sem=leave_recv.at[d],
            device_id=(my_row + d, my_col),
            device_id_type=MESH,
        )

    for d in range(1, n_row):

        @pl.when(my_row + d < n_row)
        def _():
            leave_copy(d).start()

    edge_cols[...] = jnp.zeros_like(edge_cols)

    @pl.when(has_right)
    def _():
        col_copy(True).wait_recv()
        packed = from_right[...]
        for p in range(2 * layers):
            part = pltpu.roll(packed, 128 - SUB * p, 1) if p else packed
            edge_cols[p // layers, p % layers] = jnp.where(lane < SUB, part, 0.0)

    @pl.when(has_left)
    def _():
        col_copy(False).wait_recv()
        packed = from_left[...]
        for p in range(2 * layers):
            part = pltpu.roll(packed, 128 - SUB - SUB * p, 1)
            edge_cols[p // layers, p % layers] = jnp.where(
                lane >= 128 - SUB, part, edge_cols[p // layers, p % layers]
            )

    def lateral(l, carry):
        m = jnp.concatenate([tall(0, l, slice(0, cols)), edge_cols[0, l]], 1)
        last, edge, side = cond_ref[l, rows - 8 : rows, :], edge_rows[1, l], edge_cols[1, l]
        strip = jnp.concatenate([last, edge, cond_ref[l, 0:8, :]], 0)
        low = jnp.concatenate([faces[0, l, 0 : rows - 8, :], face(strip, 0)[0:16]], 0)
        face_down = jnp.concatenate([low, face(side, 0)], 1)
        strip = jnp.concatenate(
            [cond_ref[l, :, cols - 128 : cols], side[0:rows], cond_ref[l, :, 0:128]], 1
        )
        wide = jnp.concatenate([faces[1, l, :, 0 : cols - 128], face(strip, 1)[:, 0:256]], 1)
        face_right = jnp.concatenate([wide, face(jnp.concatenate([edge, side[rows:]], 1), 1)], 0)
        for _ in range(SUB):
            flux_down = face_down * (pltpu.roll(m, height - 1, 0) - m)
            flux_right = face_right * (pltpu.roll(m, width - 1, 1) - m)
            m = m + (
                (flux_down - pltpu.roll(flux_down, 1, 0))
                + (flux_right - pltpu.roll(flux_right, 1, 1))
            )
        moved_ref[l] = m[0:rows, 0:cols]
        return carry

    lax.fori_loop(0, layers, lateral, 0)

    boundary[...] = jnp.zeros_like(boundary)
    reach_lane = lax.broadcasted_iota(jnp.int32, (128, 128), 0).astype(jnp.float32)
    row16 = lax.broadcasted_iota(jnp.int32, (16, 128), 0)
    for d in range(n_row - 1, 0, -1):

        @pl.when(my_row >= d)
        def _():
            leave_copy(d).wait_recv()
            block = met[d]
            goal = jnp.where(reach_lane == block[2:3], 1.0, 0.0).astype(jnp.bfloat16)
            flow = jnp.broadcast_to(block[0:1] * boundary[0:1] + block[1:2], (16, 128))
            first = flow.astype(jnp.bfloat16).astype(jnp.float32)
            second = (flow - first).astype(jnp.bfloat16).astype(jnp.float32)
            third = flow - first - second
            pieces = jnp.where(
                row16 == 0, first, jnp.where(row16 == 1, second, jnp.where(row16 == 2, third, 0.0))
            ).astype(jnp.bfloat16)
            got = lax.dot_general(pieces, goal, NT, preferred_element_type=jnp.float32)
            boundary[0:1] = got[0:1] + got[1:2] + got[2:3]

    enter = boundary[0:1]
    flows = [gains[i] * enter + offsets[i] for i in range(segments)]
    flow_ref[...] = jnp.concatenate(flows, 0)
    inflow_ref[...] = jnp.concatenate([enter] + flows[:-1], 0) + lateral_flow

    lists_wait(send_sem, 1, devices - 1)

    @pl.when(has_up)
    def _():
        row_copy(True).wait_send()

    @pl.when(has_down)
    def _():
        row_copy(False).wait_send()

    @pl.when(has_left)
    def _():
        col_copy(True).wait_send()

    @pl.when(has_right)
    def _():
        col_copy(False).wait_send()

    for d in range(1, n_row):

        @pl.when(my_row + d < n_row)
        def _():
            leave_copy(d).wait_send()


def exchange_step(moisture, lateral_cond, sent, reach, travel, out_b, in_b, outlet):
    layers, rows, cols = moisture.shape
    devices = sent.shape[0]
    n_row = lax.axis_size("row")
    height = rows + 8
    f32 = jnp.float32
    vmem = pl.BlockSpec(memory_space=pltpu.VMEM)
    dma = pltpu.SemaphoreType.DMA
    return pl.pallas_call(
        step_kernel,
        in_specs=[vmem] * 8,
        out_specs=[vmem] * 3,
        out_shape=[
            jax.ShapeDtypeStruct(moisture.shape, f32),
            jax.ShapeDtypeStruct(travel.shape, f32),
            jax.ShapeDtypeStruct(travel.shape, f32),
        ],
        scratch_shapes=[
            pltpu.VMEM((2, layers, 8, cols), f32),
            pltpu.VMEM((2, layers, height, 128), f32),
            pltpu.VMEM((layers, 8, cols), f32),
            pltpu.VMEM((layers, 8, cols), f32),
            pltpu.VMEM((layers, 8, cols), f32),
            pltpu.VMEM((layers, 8, cols), f32),
            pltpu.VMEM((height, 128), f32),
            pltpu.VMEM((height, 128), f32),
            pltpu.VMEM((height, 128), f32),
            pltpu.VMEM((height, 128), f32),
            pltpu.VMEM((devices, 8, 128), f32),
            pltpu.VMEM((2, layers, rows, cols), f32),
            pltpu.VMEM((8, 128), f32),
            pltpu.VMEM((n_row, 8, 128), f32),
            pltpu.VMEM((8, 128), f32),
            dma,
            dma((n_row,)),
            dma((2,)),
            dma((2,)),
            dma((2,)),
            dma((2,)),
            dma,
            dma((n_row,)),
            dma((n_row,)),
        ],
        compiler_params=pltpu.CompilerParams(
            collective_id=0, has_side_effects=True, vmem_limit_bytes=24 * 1024 * 1024
        ),
        name="exchange_step",
    )(moisture, lateral_cond, sent, reach, travel, out_b, in_b, outlet)


def finish_kernel(
    moved_ref, vert_ref, rain_ref, moist_ref, flow_in_ref, inflow_in_ref,
    new_ref, flow_ref, inflow_ref,
    solved, new_sem, flow_sem,
):
    layers, rows, _ = moved_ref.shape
    steps = rows // 8
    flow_copies = [
        pltpu.make_async_copy(flow_in_ref, flow_ref, flow_sem.at[0]),
        pltpu.make_async_copy(inflow_in_ref, inflow_ref, flow_sem.at[1]),
    ]
    for copy in flow_copies:
        copy.start()

    def new_copy(i):
        at = pl.ds(pl.multiple_of(i * 8, 8), 8)
        return pltpu.make_async_copy(solved.at[:, at, :], new_ref.at[:, at, :], new_sem.at[i])

    def solve(i, carry):
        at = pl.ds(pl.multiple_of(i * 8, 8), 8)
        upper, value = [], []
        for l in range(layers):
            v = vert_ref[l, at, :]
            right = moved_ref[l, at, :]
            if l == 0:
                wet = moist_ref[0, at, :]
                right = right + (rain_ref[at, :] - rain_ref[at, :] * (4.0 * wet * wet))
                diag = 1.0 + v
            else:
                diag = 1.0 + v + above * (1.0 - upper[-1])
                right = right + above * value[-1]
            inverse = 1.0 / diag
            upper.append(v * inverse)
            value.append(right * inverse)
            above = v
        x = value[-1]
        solved[layers - 1, at, :] = x
        for l in range(layers - 2, -1, -1):
            x = value[l] + upper[l] * x
            solved[l, at, :] = x
        new_copy(i).start()
        return carry

    lax.fori_loop(0, steps, solve, 0)
    for copy in flow_copies:
        copy.wait()
    for i in range(steps):
        new_copy(i).wait()


def finish(moved, vertical_cond, rain, moisture, flow, inflow):
    vmem = pl.BlockSpec(memory_space=pltpu.VMEM)
    out = pl.BlockSpec(memory_space=pl.ANY)
    return pl.pallas_call(
        finish_kernel,
        in_specs=[vmem] * 6,
        out_specs=[out] * 3,
        out_shape=[
            jax.ShapeDtypeStruct(moved.shape, jnp.float32),
            jax.ShapeDtypeStruct(flow.shape, jnp.float32),
            jax.ShapeDtypeStruct(flow.shape, jnp.float32),
        ],
        scratch_shapes=[
            pltpu.VMEM(moved.shape, jnp.float32),
            pltpu.SemaphoreType.DMA((moved.shape[1] // 8,)),
            pltpu.SemaphoreType.DMA((2,)),
        ],
        compiler_params=pltpu.CompilerParams(vmem_limit_bytes=16 * 1024 * 1024),
        name="finish",
    )(moved, vertical_cond, rain, moisture, flow, inflow)


def shards(
    moisture,
    lateral_cond,
    vertical_cond,
    rain,
    remap_cell,
    remap_reach,
    travel_time,
    outflow_before,
    inflow_before,
    outlet_lane,
):
    sent = look_up(moisture, vertical_cond, rain, remap_cell)
    reach = remap_reach.reshape(sent.shape)
    moved, flow, inflow = exchange_step(
        moisture, lateral_cond, sent, reach, travel_time, outflow_before, inflow_before, outlet_lane
    )
    return tuple(finish(moved, vertical_cond, rain, moisture, flow, inflow))


def solution(mesh):
    in_specs = (
        P(None, "row", "col"),
        P(None, "row", "col"),
        P(None, "row", "col"),
        P("row", "col"),
        P(("row", "col"), None, None),
        P(None, ("row", "col"), None),
        P("row", "col"),
        P("row", "col"),
        P("row", "col"),
        P("row", "col"),
    )
    out_specs = (P(None, "row", "col"), P("row", "col"), P("row", "col"))
    return jax.shard_map(shards, mesh=mesh, in_specs=in_specs, out_specs=out_specs, check_vma=False)
```

```python
import functools
import math

import jax
import jax.numpy as jnp
from jax import lax
from jax.experimental import pallas as pl
from jax.experimental.pallas import tpu as pltpu
from jax.sharding import PartitionSpec as P

SUB = 3
WEIGHT_X = 0.2
SIDEWAYS_FACTOR = 0.01

RUNOFF_LOW = 0.0025
RUNOFF_HIGH = 1.31
LOG_LOW = math.log(RUNOFF_LOW)
CODE_MAX = 65535.0
LOG_STEP = (math.log(RUNOFF_HIGH) - LOG_LOW) / CODE_MAX

BY_MATRIX = 4
UNROLL = 8
MESH = pl.DeviceIdType.MESH
NT = (((1,), (1,)), ((), ()))


def lookup_kernel(
    moist_ref, vert_ref, rain_ref, cell_ref, out_ref,
    fields, cells, table, pieces, stage, looked, counts_vec, counts, chunks, sem, fetch_sem,
):
    dests, per = cells.shape[0:2]
    last = moist_ref.shape[0] - 1
    parts = [moist_ref.at[0], moist_ref.at[last], vert_ref.at[last], rain_ref]
    field_fetches = [
        pltpu.make_async_copy(part, fields.at[i], fetch_sem.at[per + i])
        for i, part in enumerate(parts)
    ]
    for fetch in field_fetches:
        fetch.start()
    fetches = [
        pltpu.make_async_copy(
            cell_ref.at[0, :, j * 128 : (j + 1) * 128], cells.at[:, j, :], fetch_sem.at[j]
        )
        for j in range(per)
    ]
    for fetch in fetches:
        fetch.start()

    for fetch in field_fetches:
        fetch.wait()
    runoff = fields[3] * (4.0 * fields[0] * fields[0]) + fields[2] * fields[1]
    code = (jnp.log(runoff) - LOG_LOW) * (1.0 / LOG_STEP)
    code = jnp.clip(jnp.round(code), 0.0, CODE_MAX).astype(jnp.int32)
    rows = runoff.shape[0]
    for k in range(2):
        low = code[:, k * 128 : (k + 1) * 128]
        high = code[:, (k + 2) * 128 : (k + 3) * 128]
        table[k * rows : (k + 1) * rows, :] = low | (high << 16)

    turned = jnp.transpose(
        jnp.concatenate([runoff[:, k * 128 : (k + 1) * 128] for k in range(4)], 0)
    )
    first = turned.astype(jnp.bfloat16)
    pieces[0:128, :] = first
    pieces[128:256, :] = (turned - first.astype(jnp.float32)).astype(jnp.bfloat16)

    out_ref[...] = jnp.zeros_like(out_ref)
    sub = lax.broadcasted_iota(jnp.int32, (8, 128), 0)
    sub16 = lax.broadcasted_iota(jnp.int32, (16, 128), 0).astype(jnp.float32).astype(jnp.bfloat16)
    zero = jnp.zeros((16, 128), jnp.bfloat16)
    one = jnp.ones((16, 128), jnp.bfloat16)

    def row_hits(table_row, s):
        wanted = jnp.broadcast_to(table_row[s : s + 1], (16, 128)).astype(jnp.bfloat16)
        return jnp.concatenate(
            [jnp.where(sub16 + jnp.bfloat16(16 * t) == wanted, one, zero) for t in range(16)], 0
        )

    def pick_lane(found, lane):
        bits = [((lane >> b) & 1) == 1 for b in range(3, 7)]
        total = None
        for p in range(2):
            level = [found[128 * p + 8 * t : 128 * p + 8 * t + 8] for t in range(16)]
            for bit in bits:
                level = [
                    jnp.where(bit, level[2 * t + 1], level[2 * t]) for t in range(len(level) // 2)
                ]
            total = level[0] if total is None else total + level[0]
        return jnp.sum(jnp.where(sub == (lane & 7), total, 0.0), axis=0, keepdims=True)

    for fetch in fetches:
        fetch.wait()
    live = jnp.sum(jnp.where(cells[...] >= 0, 1, 0), axis=1)
    counts_vec[...] = jnp.transpose(live)[0:8, :]
    copy = pltpu.make_async_copy(counts_vec, counts, sem)
    copy.start()
    copy.wait()

    def enlist(d, total):
        for j in range(per):
            chunks[total + j] = d * per + j
        return total + counts[0, d]

    total = lax.fori_loop(0, dests, enlist, jnp.int32(0), unroll=8)
    for i in range(8 * UNROLL):
        chunks[total + i] = 0

    def step(g, carry):
        for u in range(UNROLL):
            for s in range(8):
                e = chunks[(g * UNROLL + u) * 8 + s]
                stage[u, s : s + 1, :] = cells[e >> 3, pl.ds(e & 7, 1), :]
        found = []
        for u in range(UNROLL - BY_MATRIX, UNROLL):
            cell = stage[u]
            table_row = (((cell >> 9) & 63) | ((cell >> 1) & 192)).astype(jnp.float32)
            for s in range(0, 8, 2):
                hits = jnp.concatenate([row_hits(table_row, s), row_hits(table_row, s + 1)], 1)
                found.append(jnp.dot(pieces[...], hits, preferred_element_type=jnp.float32))
        for u in range(UNROLL - BY_MATRIX):
            cell = stage[u]
            lane = cell & 127
            word_row = ((cell >> 9) & 63) | ((cell >> 1) & 64)
            odd = [None, None]
            for t in range(2 * rows):
                row = jnp.broadcast_to(table[t : t + 1, :], (8, 128))
                got = jnp.take_along_axis(row, lane, axis=1, mode="promise_in_bounds")
                old = odd[t % 2]
                odd[t % 2] = got if old is None else jnp.where(word_row == t, got, old)
            word = jnp.where((word_row & 1) == 1, odd[1], odd[0])
            half = jnp.where(((cell >> 8) & 1) == 1, word >> 16, word) & 65535
            value = jnp.exp(half.astype(jnp.float32) * LOG_STEP + LOG_LOW)
            looked[u] = jnp.where(cell >= 0, value, 0.0)
        for u in range(UNROLL - BY_MATRIX, UNROLL):
            cell = stage[u]
            for s in range(8):
                both = found[(u - UNROLL + BY_MATRIX) * 4 + s // 2]
                lane = jnp.broadcast_to(cell[s : s + 1] & 127, (8, 128))
                value = pick_lane(both[:, (s % 2) * 128 : (s % 2 + 1) * 128], lane)
                looked[u, s : s + 1, :] = jnp.where(cell[s : s + 1] >= 0, value, 0.0)
        for u in range(UNROLL):
            for s in range(8):
                e = chunks[(g * UNROLL + u) * 8 + s]
                out_ref[e >> 3, pl.ds(e & 7, 1), :] = looked[u, s : s + 1, :]
        return carry

    lax.fori_loop(0, (total + (8 * UNROLL - 1)) // (8 * UNROLL), step, 0)


def look_up(moisture, vertical_cond, rain, remap_cell):
    layers, rows, cols = moisture.shape
    dests, slots = remap_cell.shape[1:]
    return pl.pallas_call(
        lookup_kernel,
        in_specs=[pl.BlockSpec(memory_space=pltpu.HBM)] * 4,
        out_specs=pl.BlockSpec(memory_space=pltpu.VMEM),
        out_shape=jax.ShapeDtypeStruct((dests, slots // 128, 128), jnp.float32),
        scratch_shapes=[
            pltpu.VMEM((4, rows, cols), jnp.float32),
            pltpu.VMEM((dests, slots // 128, 128), jnp.int32),
            pltpu.VMEM((2 * rows, 128), jnp.int32),
            pltpu.VMEM((256, 4 * rows), jnp.bfloat16),
            pltpu.VMEM((UNROLL, 8, 128), jnp.int32),
            pltpu.VMEM((UNROLL, 8, 128), jnp.float32),
            pltpu.VMEM((8, dests), jnp.int32),
            pltpu.SMEM((8, dests), jnp.int32),
            pltpu.SMEM((dests * (slots // 128) + 8 * UNROLL + 8,), jnp.int32),
            pltpu.SemaphoreType.DMA,
            pltpu.SemaphoreType.DMA((slots // 128 + 4,)),
        ],
        compiler_params=pltpu.CompilerParams(vmem_limit_bytes=53 * 1024 * 1024),
        name="look_up",
    )(moisture, vertical_cond, rain, remap_cell)


HALF_BINS = 64


def step_kernel(
    moist_ref, cond_ref, sent_ref, reach_ref,
    travel_ref, out_before_ref, in_before_ref, outlet_ref,
    moved_ref, flow_ref, inflow_ref,
    edge_rows, edge_cols, pack_up, pack_down, below, above, pack_left, pack_right, from_right, from_left,
    arrived, faces, leave, met, boundary,
    send_sem, recv_sem, row_send, row_recv, col_send, col_recv, own_sem, leave_send, leave_recv,
):
    n_row, n_col = lax.axis_size("row"), lax.axis_size("col")
    devices = n_row * n_col
    my_row, my_col = lax.axis_index("row"), lax.axis_index("col")
    me = my_row * n_col + my_col
    layers, rows, cols = moist_ref.shape
    height, width = rows + 8, cols + 128
    fields = (moist_ref, cond_ref)

    barrier = pltpu.get_barrier_semaphore()

    def wrap(x, size):
        return jnp.where(x >= size, x - size, x)

    ahead = [wrap(my_col + dc, n_col) for dc in range(n_col)]
    behind = [wrap(my_col + n_col - dc, n_col) for dc in range(n_col)]

    def greet(dr, first):
        row = wrap(my_row + dr, n_row)
        for dc in range(first, n_col):
            pl.semaphore_signal(
                barrier, inc=1, device_id=(row, ahead[dc]), device_id_type=MESH
            )

    greet(0, 1)

    @pl.loop(1, n_row)
    def _(dr):
        greet(dr, 0)

    travel = travel_ref[...]
    denom = 1.0 / (1.0 + 2.0 * travel * (1.0 - WEIGHT_X))
    gain = (1.0 - 2.0 * travel * WEIGHT_X) * denom
    rest = (1.0 + 2.0 * travel * WEIGHT_X) * denom * in_before_ref[...]
    rest += (2.0 * travel * (1.0 - WEIGHT_X) - 1.0) * denom * out_before_ref[...]

    has_up, has_down = my_row > 0, my_row < n_row - 1
    has_left, has_right = my_col > 0, my_col < n_col - 1

    sub = lax.broadcasted_iota(jnp.int32, (layers, 8, cols), 1)
    pack_up[...] = jnp.where(
        sub < SUB, moist_ref[:, 0:8, :], pltpu.roll(cond_ref[:, 0:8, :], 8 - SUB, 1)
    )
    pack_down[...] = jnp.where(
        sub >= 8 - SUB,
        moist_ref[:, rows - 8 : rows, :],
        pltpu.roll(cond_ref[:, rows - 8 : rows, :], SUB, 1),
    )

    def row_copy(up):
        return pltpu.make_async_remote_copy(
            src_ref=pack_up if up else pack_down,
            dst_ref=below if up else above,
            send_sem=row_send.at[0 if up else 1],
            recv_sem=row_recv.at[0 if up else 1],
            device_id=(my_row - 1 if up else my_row + 1, my_col),
            device_id_type=MESH,
        )

    pl.semaphore_wait(barrier, devices - 1)

    def send_lists(dr, first):
        row = wrap(my_row + dr, n_row)
        for dc in range(first, n_col):
            pltpu.make_async_remote_copy(
                src_ref=sent_ref.at[row * n_col + ahead[dc]],
                dst_ref=arrived.at[dr * n_col + dc],
                send_sem=send_sem,
                recv_sem=recv_sem.at[dr],
                device_id=(row, ahead[dc]),
                device_id_type=MESH,
            ).start()

    send_lists(0, 1)

    @pl.loop(1, n_row)
    def _(dr):
        send_lists(dr, 0)

    def lists_wait(sem, first, count):
        place = arrived.at[pl.ds(first, count)]
        pltpu.make_async_copy(place, place, sem).wait()

    @pl.when(has_up)
    def _():
        row_copy(True).start()

    @pl.when(has_down)
    def _():
        row_copy(False).start()

    own = pltpu.make_async_copy(sent_ref.at[me], arrived.at[0], own_sem)
    own.start()

    def face(c, axis):
        size = c.shape[axis]
        near = pltpu.roll(c, size - 1, axis)
        return 2.0 * c * near / jnp.maximum(c + near, 1e-30)

    def inner_faces(l, carry):
        c = cond_ref[l]
        faces[0, l] = face(c, 0)
        faces[1, l] = face(c, 1)
        return carry

    lax.fori_loop(0, layers, inner_faces, 0)

    own.wait()
    base = lax.broadcasted_iota(jnp.int32, (16, 1024), 0).astype(jnp.float32).astype(jnp.bfloat16)
    zero = jnp.zeros((16, 1024), jnp.bfloat16)
    one = jnp.ones((16, 1024), jnp.bfloat16)

    def spread(x):
        return jnp.concatenate(
            [jnp.broadcast_to(x[j : j + 1, :], (16, 128)).astype(jnp.bfloat16) for j in range(8)], 1
        )

    def add_up(dr, acc):
        row = wrap(my_row + n_row - dr, n_row)
        for dc in range(n_col):
            k = dr * n_col + dc
            q = reach_ref[row * n_col + behind[dc]]
            value = arrived[k]
            first = value.astype(jnp.bfloat16).astype(jnp.float32)
            head, tail = spread(first), spread(value - first)
            a = spread(((q >> 7) + 16 * ((q >> 6) & 1)).astype(jnp.float32))
            b = spread((q & 63).astype(jnp.float32))
            hits = [base + jnp.bfloat16(16 * t) == a for t in range(2)]
            values = jnp.concatenate(
                [jnp.where(h, head, zero) for h in hits] + [jnp.where(h, tail, zero) for h in hits], 0
            )
            places = jnp.concatenate(
                [jnp.where(base + jnp.bfloat16(16 * t) == b, one, zero) for t in range(4)], 0
            )
            acc = acc + lax.dot_general(values, places, NT, preferred_element_type=jnp.float32)
        return acc

    def wait_and_add(dr, acc):
        lists_wait(recv_sem.at[dr], dr * n_col, n_col)
        return add_up(dr, acc)

    lists_wait(recv_sem.at[0], 1, n_col - 1)
    bins = add_up(0, jnp.zeros((64, HALF_BINS), jnp.float32))
    bins = lax.fori_loop(1, n_row // 2, wait_and_add, bins)

    edge_rows[...] = jnp.zeros_like(edge_rows)

    @pl.when(has_down)
    def _():
        row_copy(True).wait_recv()
        edge_rows[0] = jnp.where(sub < SUB, below[...], 0.0)
        edge_rows[1] = jnp.where(sub < SUB, pltpu.roll(below[...], SUB, 1), 0.0)

    @pl.when(has_up)
    def _():
        row_copy(False).wait_recv()
        edge_rows[0] = jnp.where(sub >= 8 - SUB, above[...], edge_rows[0])
        edge_rows[1] = jnp.where(sub >= 8 - SUB, pltpu.roll(above[...], 8 - SUB, 1), edge_rows[1])

    def tall(f, l, lanes):
        return jnp.concatenate([fields[f][l, :, lanes], edge_rows[f, l, :, lanes]], 0)

    lane = lax.broadcasted_iota(jnp.int32, (height, 128), 1)
    left_pack = jnp.zeros((height, 128), jnp.float32)
    right_pack = jnp.zeros((height, 128), jnp.float32)
    for p in range(2 * layers):
        here = (lane >= SUB * p) & (lane < SUB * (p + 1))
        first = tall(p // layers, p % layers, slice(0, 128))
        last = tall(p // layers, p % layers, slice(cols - 128, cols))
        left_pack = jnp.where(here, pltpu.roll(first, SUB * p, 1) if p else first, left_pack)
        right_pack = jnp.where(here, pltpu.roll(last, SUB * p + SUB, 1), right_pack)
    pack_left[...] = left_pack
    pack_right[...] = right_pack

    def col_copy(left):
        return pltpu.make_async_remote_copy(
            src_ref=pack_left if left else pack_right,
            dst_ref=from_right if left else from_left,
            send_sem=col_send.at[0 if left else 1],
            recv_sem=col_recv.at[0 if left else 1],
            device_id=(my_row, my_col - 1 if left else my_col + 1),
            device_id_type=MESH,
        )

    @pl.when(has_left)
    def _():
        col_copy(True).start()

    @pl.when(has_right)
    def _():
        col_copy(False).start()

    bins = lax.fori_loop(n_row // 2, n_row, wait_and_add, bins)
    bins = SIDEWAYS_FACTOR * (bins[0:32] + bins[32:64])
    lateral_flow = jnp.concatenate([bins[0:16], bins[16:32]], 1)

    segments = lateral_flow.shape[0]
    offset_term = gain * lateral_flow + rest
    gains, offsets = [gain[0:1]], [offset_term[0:1]]
    for i in range(1, segments):
        g = gain[i : i + 1]
        gains.append(g * gains[-1])
        offsets.append(g * offsets[-1] + offset_term[i : i + 1])

    leave[0:1] = gains[-1]
    leave[1:2] = offsets[-1]
    leave[2:3] = outlet_ref[...].astype(jnp.float32)
    leave[3:8] = jnp.zeros((5, leave.shape[1]), jnp.float32)

    def leave_copy(d):
        return pltpu.make_async_remote_copy(
            src_ref=leave,
            dst_ref=met.at[d],
            send_sem=leave_send.at[d],
            recv_sem=leave_recv.at[d],
            device_id=(my_row + d, my_col),
            device_id_type=MESH,
        )

    for d in range(1, n_row):

        @pl.when(my_row + d < n_row)
        def _():
            leave_copy(d).start()

    edge_cols[...] = jnp.zeros_like(edge_cols)

    @pl.when(has_right)
    def _():
        col_copy(True).wait_recv()
        packed = from_right[...]
        for p in range(2 * layers):
            part = pltpu.roll(packed, 128 - SUB * p, 1) if p else packed
            edge_cols[p // layers, p % layers] = jnp.where(lane < SUB, part, 0.0)

    @pl.when(has_left)
    def _():
        col_copy(False).wait_recv()
        packed = from_left[...]
        for p in range(2 * layers):
            part = pltpu.roll(packed, 128 - SUB - SUB * p, 1)
            edge_cols[p // layers, p % layers] = jnp.where(
                lane >= 128 - SUB, part, edge_cols[p // layers, p % layers]
            )

    def lateral(l, carry):
        m = jnp.concatenate([tall(0, l, slice(0, cols)), edge_cols[0, l]], 1)
        last, edge, side = cond_ref[l, rows - 8 : rows, :], edge_rows[1, l], edge_cols[1, l]
        strip = jnp.concatenate([last, edge, cond_ref[l, 0:8, :]], 0)
        low = jnp.concatenate([faces[0, l, 0 : rows - 8, :], face(strip, 0)[0:16]], 0)
        face_down = jnp.concatenate([low, face(side, 0)], 1)
        strip = jnp.concatenate(
            [cond_ref[l, :, cols - 128 : cols], side[0:rows], cond_ref[l, :, 0:128]], 1
        )
        wide = jnp.concatenate([faces[1, l, :, 0 : cols - 128], face(strip, 1)[:, 0:256]], 1)
        face_right = jnp.concatenate([wide, face(jnp.concatenate([edge, side[rows:]], 1), 1)], 0)
        for _ in range(SUB):
            flux_down = face_down * (pltpu.roll(m, height - 1, 0) - m)
            flux_right = face_right * (pltpu.roll(m, width - 1, 1) - m)
            m = m + (
                (flux_down - pltpu.roll(flux_down, 1, 0))
                + (flux_right - pltpu.roll(flux_right, 1, 1))
            )
        moved_ref[l] = m[0:rows, 0:cols]
        return carry

    lax.fori_loop(0, layers, lateral, 0)

    boundary[...] = jnp.zeros_like(boundary)
    reach_lane = lax.broadcasted_iota(jnp.int32, (128, 128), 0).astype(jnp.float32)
    row16 = lax.broadcasted_iota(jnp.int32, (16, 128), 0)
    for d in range(n_row - 1, 0, -1):

        @pl.when(my_row >= d)
        def _():
            leave_copy(d).wait_recv()
            block = met[d]
            goal = jnp.where(reach_lane == block[2:3], 1.0, 0.0).astype(jnp.bfloat16)
            flow = jnp.broadcast_to(block[0:1] * boundary[0:1] + block[1:2], (16, 128))
            first = flow.astype(jnp.bfloat16).astype(jnp.float32)
            second = (flow - first).astype(jnp.bfloat16).astype(jnp.float32)
            third = flow - first - second
            pieces = jnp.where(
                row16 == 0, first, jnp.where(row16 == 1, second, jnp.where(row16 == 2, third, 0.0))
            ).astype(jnp.bfloat16)
            got = lax.dot_general(pieces, goal, NT, preferred_element_type=jnp.float32)
            boundary[0:1] = got[0:1] + got[1:2] + got[2:3]

    enter = boundary[0:1]
    flows = [gains[i] * enter + offsets[i] for i in range(segments)]
    flow_ref[...] = jnp.concatenate(flows, 0)
    inflow_ref[...] = jnp.concatenate([enter] + flows[:-1], 0) + lateral_flow

    lists_wait(send_sem, 1, devices - 1)

    @pl.when(has_up)
    def _():
        row_copy(True).wait_send()

    @pl.when(has_down)
    def _():
        row_copy(False).wait_send()

    @pl.when(has_left)
    def _():
        col_copy(True).wait_send()

    @pl.when(has_right)
    def _():
        col_copy(False).wait_send()

    for d in range(1, n_row):

        @pl.when(my_row + d < n_row)
        def _():
            leave_copy(d).wait_send()


def exchange_step(moisture, lateral_cond, sent, reach, travel, out_b, in_b, outlet):
    layers, rows, cols = moisture.shape
    devices = sent.shape[0]
    n_row = lax.axis_size("row")
    height = rows + 8
    f32 = jnp.float32
    vmem = pl.BlockSpec(memory_space=pltpu.VMEM)
    dma = pltpu.SemaphoreType.DMA
    return pl.pallas_call(
        step_kernel,
        in_specs=[vmem] * 8,
        out_specs=[vmem] * 3,
        out_shape=[
            jax.ShapeDtypeStruct(moisture.shape, f32),
            jax.ShapeDtypeStruct(travel.shape, f32),
            jax.ShapeDtypeStruct(travel.shape, f32),
        ],
        scratch_shapes=[
            pltpu.VMEM((2, layers, 8, cols), f32),
            pltpu.VMEM((2, layers, height, 128), f32),
            pltpu.VMEM((layers, 8, cols), f32),
            pltpu.VMEM((layers, 8, cols), f32),
            pltpu.VMEM((layers, 8, cols), f32),
            pltpu.VMEM((layers, 8, cols), f32),
            pltpu.VMEM((height, 128), f32),
            pltpu.VMEM((height, 128), f32),
            pltpu.VMEM((height, 128), f32),
            pltpu.VMEM((height, 128), f32),
            pltpu.VMEM((devices, 8, 128), f32),
            pltpu.VMEM((2, layers, rows, cols), f32),
            pltpu.VMEM((8, 128), f32),
            pltpu.VMEM((n_row, 8, 128), f32),
            pltpu.VMEM((8, 128), f32),
            dma,
            dma((n_row,)),
            dma((2,)),
            dma((2,)),
            dma((2,)),
            dma((2,)),
            dma,
            dma((n_row,)),
            dma((n_row,)),
        ],
        compiler_params=pltpu.CompilerParams(
            collective_id=0, has_side_effects=True, vmem_limit_bytes=24 * 1024 * 1024
        ),
        name="exchange_step",
    )(moisture, lateral_cond, sent, reach, travel, out_b, in_b, outlet)


def finish_kernel(
    moved_ref, vert_ref, rain_ref, moist_ref, flow_in_ref, inflow_in_ref,
    new_ref, flow_ref, inflow_ref,
    solved, new_sem, flow_sem,
):
    layers, rows, _ = moved_ref.shape
    steps = rows // 8
    flow_copies = [
        pltpu.make_async_copy(flow_in_ref, flow_ref, flow_sem.at[0]),
        pltpu.make_async_copy(inflow_in_ref, inflow_ref, flow_sem.at[1]),
    ]
    for copy in flow_copies:
        copy.start()

    def new_copy(i):
        at = pl.ds(pl.multiple_of(i * 8, 8), 8)
        return pltpu.make_async_copy(solved.at[:, at, :], new_ref.at[:, at, :], new_sem.at[i])

    def solve(i, carry):
        at = pl.ds(pl.multiple_of(i * 8, 8), 8)
        upper, value = [], []
        for l in range(layers):
            v = vert_ref[l, at, :]
            right = moved_ref[l, at, :]
            if l == 0:
                wet = moist_ref[0, at, :]
                right = right + (rain_ref[at, :] - rain_ref[at, :] * (4.0 * wet * wet))
                diag = 1.0 + v
            else:
                diag = 1.0 + v + above * (1.0 - upper[-1])
                right = right + above * value[-1]
            inverse = 1.0 / diag
            upper.append(v * inverse)
            value.append(right * inverse)
            above = v
        x = value[-1]
        solved[layers - 1, at, :] = x
        for l in range(layers - 2, -1, -1):
            x = value[l] + upper[l] * x
            solved[l, at, :] = x
        new_copy(i).start()
        return carry

    lax.fori_loop(0, steps, solve, 0)
    for copy in flow_copies:
        copy.wait()
    for i in range(steps):
        new_copy(i).wait()


def finish(moved, vertical_cond, rain, moisture, flow, inflow):
    vmem = pl.BlockSpec(memory_space=pltpu.VMEM)
    out = pl.BlockSpec(memory_space=pl.ANY)
    return pl.pallas_call(
        finish_kernel,
        in_specs=[vmem] * 6,
        out_specs=[out] * 3,
        out_shape=[
            jax.ShapeDtypeStruct(moved.shape, jnp.float32),
            jax.ShapeDtypeStruct(flow.shape, jnp.float32),
            jax.ShapeDtypeStruct(flow.shape, jnp.float32),
        ],
        scratch_shapes=[
            pltpu.VMEM(moved.shape, jnp.float32),
            pltpu.SemaphoreType.DMA((moved.shape[1] // 8,)),
            pltpu.SemaphoreType.DMA((2,)),
        ],
        compiler_params=pltpu.CompilerParams(vmem_limit_bytes=16 * 1024 * 1024),
        name="finish",
    )(moved, vertical_cond, rain, moisture, flow, inflow)


def shards(
    moisture,
    lateral_cond,
    vertical_cond,
    rain,
    remap_cell,
    remap_reach,
    travel_time,
    outflow_before,
    inflow_before,
    outlet_lane,
):
    sent = look_up(moisture, vertical_cond, rain, remap_cell)
    reach = remap_reach.reshape(sent.shape)
    moved, flow, inflow = exchange_step(
        moisture, lateral_cond, sent, reach, travel_time, outflow_before, inflow_before, outlet_lane
    )
    return tuple(finish(moved, vertical_cond, rain, moisture, flow, inflow))


def solution(mesh):
    in_specs = (
        P(None, "row", "col"),
        P(None, "row", "col"),
        P(None, "row", "col"),
        P("row", "col"),
        P(("row", "col"), None, None),
        P(None, ("row", "col"), None),
        P("row", "col"),
        P("row", "col"),
        P("row", "col"),
        P("row", "col"),
    )
    out_specs = (P(None, "row", "col"), P("row", "col"), P("row", "col"))
    return jax.shard_map(shards, mesh=mesh, in_specs=in_specs, out_specs=out_specs, check_vma=False)
```

```python
import functools
import math

import jax
import jax.numpy as jnp
from jax import lax
from jax.experimental import pallas as pl
from jax.experimental.pallas import tpu as pltpu
from jax.sharding import PartitionSpec as P

SUB = 3
WEIGHT_X = 0.2
SIDEWAYS_FACTOR = 0.01

RUNOFF_LOW = 0.0025
RUNOFF_HIGH = 1.31
LOG_LOW = math.log(RUNOFF_LOW)
CODE_MAX = 65535.0
LOG_STEP = (math.log(RUNOFF_HIGH) - LOG_LOW) / CODE_MAX

BY_MATRIX = 4
UNROLL = 8
MESH = pl.DeviceIdType.MESH
NT = (((1,), (1,)), ((), ()))


def lookup_kernel(
    moist_ref, vert_ref, rain_ref, cell_ref, out_ref,
    fields, cells, table, pieces, stage, looked, counts_vec, counts, chunks, sem, fetch_sem,
):
    dests, per = cells.shape[0:2]
    last = moist_ref.shape[0] - 1
    parts = [moist_ref.at[0], moist_ref.at[last], vert_ref.at[last], rain_ref]
    field_fetches = [
        pltpu.make_async_copy(part, fields.at[i], fetch_sem.at[per + i])
        for i, part in enumerate(parts)
    ]
    for fetch in field_fetches:
        fetch.start()
    fetches = [
        pltpu.make_async_copy(
            cell_ref.at[0, :, j * 128 : (j + 1) * 128], cells.at[:, j, :], fetch_sem.at[j]
        )
        for j in range(per)
    ]
    for fetch in fetches:
        fetch.start()

    for fetch in field_fetches:
        fetch.wait()
    runoff = fields[3] * (4.0 * fields[0] * fields[0]) + fields[2] * fields[1]
    code = (jnp.log(runoff) - LOG_LOW) * (1.0 / LOG_STEP)
    code = jnp.clip(jnp.round(code), 0.0, CODE_MAX).astype(jnp.int32)
    rows = runoff.shape[0]
    for k in range(2):
        low = code[:, k * 128 : (k + 1) * 128]
        high = code[:, (k + 2) * 128 : (k + 3) * 128]
        table[k * rows : (k + 1) * rows, :] = low | (high << 16)

    turned = jnp.transpose(
        jnp.concatenate([runoff[:, k * 128 : (k + 1) * 128] for k in range(4)], 0)
    )
    first = turned.astype(jnp.bfloat16)
    pieces[0:128, :] = first
    pieces[128:256, :] = (turned - first.astype(jnp.float32)).astype(jnp.bfloat16)

    out_ref[...] = jnp.zeros_like(out_ref)
    sub = lax.broadcasted_iota(jnp.int32, (8, 128), 0)
    sub16 = lax.broadcasted_iota(jnp.int32, (16, 128), 0).astype(jnp.float32).astype(jnp.bfloat16)
    zero = jnp.zeros((16, 128), jnp.bfloat16)
    one = jnp.ones((16, 128), jnp.bfloat16)

    def row_hits(table_row, s):
        wanted = jnp.broadcast_to(table_row[s : s + 1], (16, 128)).astype(jnp.bfloat16)
        return jnp.concatenate(
            [jnp.where(sub16 + jnp.bfloat16(16 * t) == wanted, one, zero) for t in range(16)], 0
        )

    def pick_lane(found, lane):
        bits = [((lane >> b) & 1) == 1 for b in range(3, 7)]
        total = None
        for p in range(2):
            level = [found[128 * p + 8 * t : 128 * p + 8 * t + 8] for t in range(16)]
            for bit in bits:
                level = [
                    jnp.where(bit, level[2 * t + 1], level[2 * t]) for t in range(len(level) // 2)
                ]
            total = level[0] if total is None else total + level[0]
        return jnp.sum(jnp.where(sub == (lane & 7), total, 0.0), axis=0, keepdims=True)

    for fetch in fetches:
        fetch.wait()
    live = jnp.sum(jnp.where(cells[...] >= 0, 1, 0), axis=1)
    counts_vec[...] = jnp.transpose(live)[0:8, :]
    copy = pltpu.make_async_copy(counts_vec, counts, sem)
    copy.start()
    copy.wait()

    def enlist(d, total):
        for j in range(per):
            chunks[total + j] = d * per + j
        return total + counts[0, d]

    total = lax.fori_loop(0, dests, enlist, jnp.int32(0), unroll=8)
    for i in range(8 * UNROLL):
        chunks[total + i] = 0

    def step(g, carry):
        for u in range(UNROLL):
            for s in range(8):
                e = chunks[(g * UNROLL + u) * 8 + s]
                stage[u, s : s + 1, :] = cells[e >> 3, pl.ds(e & 7, 1), :]
        found = []
        for u in range(UNROLL - BY_MATRIX, UNROLL):
            cell = stage[u]
            table_row = (((cell >> 9) & 63) | ((cell >> 1) & 192)).astype(jnp.float32)
            for s in range(0, 8, 2):
                hits = jnp.concatenate([row_hits(table_row, s), row_hits(table_row, s + 1)], 1)
                found.append(jnp.dot(pieces[...], hits, preferred_element_type=jnp.float32))
        for u in range(UNROLL - BY_MATRIX):
            cell = stage[u]
            lane = cell & 127
            word_row = ((cell >> 9) & 63) | ((cell >> 1) & 64)
            odd = [None, None]
            for t in range(2 * rows):
                row = jnp.broadcast_to(table[t : t + 1, :], (8, 128))
                got = jnp.take_along_axis(row, lane, axis=1, mode="promise_in_bounds")
                old = odd[t % 2]
                odd[t % 2] = got if old is None else jnp.where(word_row == t, got, old)
            word = jnp.where((word_row & 1) == 1, odd[1], odd[0])
            half = jnp.where(((cell >> 8) & 1) == 1, word >> 16, word) & 65535
            value = jnp.exp(half.astype(jnp.float32) * LOG_STEP + LOG_LOW)
            looked[u] = jnp.where(cell >= 0, value, 0.0)
        for u in range(UNROLL - BY_MATRIX, UNROLL):
            cell = stage[u]
            for s in range(8):
                both = found[(u - UNROLL + BY_MATRIX) * 4 + s // 2]
                lane = jnp.broadcast_to(cell[s : s + 1] & 127, (8, 128))
                value = pick_lane(both[:, (s % 2) * 128 : (s % 2 + 1) * 128], lane)
                looked[u, s : s + 1, :] = jnp.where(cell[s : s + 1] >= 0, value, 0.0)
        for u in range(UNROLL):
            for s in range(8):
                e = chunks[(g * UNROLL + u) * 8 + s]
                out_ref[e >> 3, pl.ds(e & 7, 1), :] = looked[u, s : s + 1, :]
        return carry

    lax.fori_loop(0, (total + (8 * UNROLL - 1)) // (8 * UNROLL), step, 0)


def look_up(moisture, vertical_cond, rain, remap_cell):
    layers, rows, cols = moisture.shape
    dests, slots = remap_cell.shape[1:]
    return pl.pallas_call(
        lookup_kernel,
        in_specs=[pl.BlockSpec(memory_space=pltpu.HBM)] * 4,
        out_specs=pl.BlockSpec(memory_space=pltpu.VMEM),
        out_shape=jax.ShapeDtypeStruct((dests, slots // 128, 128), jnp.float32),
        scratch_shapes=[
            pltpu.VMEM((4, rows, cols), jnp.float32),
            pltpu.VMEM((dests, slots // 128, 128), jnp.int32),
            pltpu.VMEM((2 * rows, 128), jnp.int32),
            pltpu.VMEM((256, 4 * rows), jnp.bfloat16),
            pltpu.VMEM((UNROLL, 8, 128), jnp.int32),
            pltpu.VMEM((UNROLL, 8, 128), jnp.float32),
            pltpu.VMEM((8, dests), jnp.int32),
            pltpu.SMEM((8, dests), jnp.int32),
            pltpu.SMEM((dests * (slots // 128) + 8 * UNROLL + 8,), jnp.int32),
            pltpu.SemaphoreType.DMA,
            pltpu.SemaphoreType.DMA((slots // 128 + 4,)),
        ],
        compiler_params=pltpu.CompilerParams(vmem_limit_bytes=53 * 1024 * 1024),
        name="look_up",
    )(moisture, vertical_cond, rain, remap_cell)


HALF_BINS = 64


def step_kernel(
    moist_ref, cond_ref, sent_ref, reach_ref,
    travel_ref, out_before_ref, in_before_ref, outlet_ref,
    moved_ref, flow_ref, inflow_ref,
    edge_rows, edge_cols, pack_up, pack_down, below, above, pack_left, pack_right, from_right, from_left,
    arrived, faces, leave, met, boundary,
    send_sem, recv_sem, row_send, row_recv, col_send, col_recv, own_sem, leave_send, leave_recv,
):
    n_row, n_col = lax.axis_size("row"), lax.axis_size("col")
    devices = n_row * n_col
    my_row, my_col = lax.axis_index("row"), lax.axis_index("col")
    me = my_row * n_col + my_col
    layers, rows, cols = moist_ref.shape
    height, width = rows + 8, cols + 128
    fields = (moist_ref, cond_ref)

    barrier = pltpu.get_barrier_semaphore()

    def wrap(x, size):
        return jnp.where(x >= size, x - size, x)

    ahead = [wrap(my_col + dc, n_col) for dc in range(n_col)]
    behind = [wrap(my_col + n_col - dc, n_col) for dc in range(n_col)]

    def greet(dr, first):
        row = wrap(my_row + dr, n_row)
        for dc in range(first, n_col):
            pl.semaphore_signal(
                barrier, inc=1, device_id=(row, ahead[dc]), device_id_type=MESH
            )

    greet(0, 1)

    @pl.loop(1, n_row)
    def _(dr):
        greet(dr, 0)

    travel = travel_ref[...]
    denom = 1.0 / (1.0 + 2.0 * travel * (1.0 - WEIGHT_X))
    gain = (1.0 - 2.0 * travel * WEIGHT_X) * denom
    rest = (1.0 + 2.0 * travel * WEIGHT_X) * denom * in_before_ref[...]
    rest += (2.0 * travel * (1.0 - WEIGHT_X) - 1.0) * denom * out_before_ref[...]

    has_up, has_down = my_row > 0, my_row < n_row - 1
    has_left, has_right = my_col > 0, my_col < n_col - 1

    sub = lax.broadcasted_iota(jnp.int32, (layers, 8, cols), 1)
    pack_up[...] = jnp.where(
        sub < SUB, moist_ref[:, 0:8, :], pltpu.roll(cond_ref[:, 0:8, :], 8 - SUB, 1)
    )
    pack_down[...] = jnp.where(
        sub >= 8 - SUB,
        moist_ref[:, rows - 8 : rows, :],
        pltpu.roll(cond_ref[:, rows - 8 : rows, :], SUB, 1),
    )

    def row_copy(up):
        return pltpu.make_async_remote_copy(
            src_ref=pack_up if up else pack_down,
            dst_ref=below if up else above,
            send_sem=row_send.at[0 if up else 1],
            recv_sem=row_recv.at[0 if up else 1],
            device_id=(my_row - 1 if up else my_row + 1, my_col),
            device_id_type=MESH,
        )

    pl.semaphore_wait(barrier, devices - 1)

    def send_lists(dr, first):
        row = wrap(my_row + dr, n_row)
        for dc in range(first, n_col):
            pltpu.make_async_remote_copy(
                src_ref=sent_ref.at[row * n_col + ahead[dc]],
                dst_ref=arrived.at[dr * n_col + dc],
                send_sem=send_sem,
                recv_sem=recv_sem.at[dr],
                device_id=(row, ahead[dc]),
                device_id_type=MESH,
            ).start()

    send_lists(0, 1)

    @pl.loop(1, n_row)
    def _(dr):
        send_lists(dr, 0)

    def lists_wait(sem, first, count):
        place = arrived.at[pl.ds(first, count)]
        pltpu.make_async_copy(place, place, sem).wait()

    @pl.when(has_up)
    def _():
        row_copy(True).start()

    @pl.when(has_down)
    def _():
        row_copy(False).start()

    own = pltpu.make_async_copy(sent_ref.at[me], arrived.at[0], own_sem)
    own.start()

    def face(c, axis):
        size = c.shape[axis]
        near = pltpu.roll(c, size - 1, axis)
        return 2.0 * c * near / jnp.maximum(c + near, 1e-30)

    def inner_faces(l, carry):
        c = cond_ref[l]
        faces[0, l] = face(c, 0)
        faces[1, l] = face(c, 1)
        return carry

    lax.fori_loop(0, layers, inner_faces, 0)

    own.wait()
    base = lax.broadcasted_iota(jnp.int32, (16, 1024), 0).astype(jnp.float32).astype(jnp.bfloat16)
    zero = jnp.zeros((16, 1024), jnp.bfloat16)
    one = jnp.ones((16, 1024), jnp.bfloat16)

    def spread(x):
        return jnp.concatenate(
            [jnp.broadcast_to(x[j : j + 1, :], (16, 128)).astype(jnp.bfloat16) for j in range(8)], 1
        )

    def add_up(dr, acc):
        row = wrap(my_row + n_row - dr, n_row)
        for dc in range(n_col):
            k = dr * n_col + dc
            q = reach_ref[row * n_col + behind[dc]]
            value = arrived[k]
            first = value.astype(jnp.bfloat16).astype(jnp.float32)
            head, tail = spread(first), spread(value - first)
            a = spread(((q >> 7) + 16 * ((q >> 6) & 1)).astype(jnp.float32))
            b = spread((q & 63).astype(jnp.float32))
            hits = [base + jnp.bfloat16(16 * t) == a for t in range(2)]
            values = jnp.concatenate(
                [jnp.where(h, head, zero) for h in hits] + [jnp.where(h, tail, zero) for h in hits], 0
            )
            places = jnp.concatenate(
                [jnp.where(base + jnp.bfloat16(16 * t) == b, one, zero) for t in range(4)], 0
            )
            acc = acc + lax.dot_general(values, places, NT, preferred_element_type=jnp.float32)
        return acc

    def wait_and_add(dr, acc):
        lists_wait(recv_sem.at[dr], dr * n_col, n_col)
        return add_up(dr, acc)

    lists_wait(recv_sem.at[0], 1, n_col - 1)
    bins = add_up(0, jnp.zeros((64, HALF_BINS), jnp.float32))
    bins = lax.fori_loop(1, n_row // 2, wait_and_add, bins)

    edge_rows[...] = jnp.zeros_like(edge_rows)

    @pl.when(has_down)
    def _():
        row_copy(True).wait_recv()
        edge_rows[0] = jnp.where(sub < SUB, below[...], 0.0)
        edge_rows[1] = jnp.where(sub < SUB, pltpu.roll(below[...], SUB, 1), 0.0)

    @pl.when(has_up)
    def _():
        row_copy(False).wait_recv()
        edge_rows[0] = jnp.where(sub >= 8 - SUB, above[...], edge_rows[0])
        edge_rows[1] = jnp.where(sub >= 8 - SUB, pltpu.roll(above[...], 8 - SUB, 1), edge_rows[1])

    def tall(f, l, lanes):
        return jnp.concatenate([fields[f][l, :, lanes], edge_rows[f, l, :, lanes]], 0)

    lane = lax.broadcasted_iota(jnp.int32, (height, 128), 1)
    left_pack = jnp.zeros((height, 128), jnp.float32)
    right_pack = jnp.zeros((height, 128), jnp.float32)
    for p in range(2 * layers):
        here = (lane >= SUB * p) & (lane < SUB * (p + 1))
        first = tall(p // layers, p % layers, slice(0, 128))
        last = tall(p // layers, p % layers, slice(cols - 128, cols))
        left_pack = jnp.where(here, pltpu.roll(first, SUB * p, 1) if p else first, left_pack)
        right_pack = jnp.where(here, pltpu.roll(last, SUB * p + SUB, 1), right_pack)
    pack_left[...] = left_pack
    pack_right[...] = right_pack

    def col_copy(left):
        return pltpu.make_async_remote_copy(
            src_ref=pack_left if left else pack_right,
            dst_ref=from_right if left else from_left,
            send_sem=col_send.at[0 if left else 1],
            recv_sem=col_recv.at[0 if left else 1],
            device_id=(my_row, my_col - 1 if left else my_col + 1),
            device_id_type=MESH,
        )

    @pl.when(has_left)
    def _():
        col_copy(True).start()

    @pl.when(has_right)
    def _():
        col_copy(False).start()

    bins = lax.fori_loop(n_row // 2, n_row, wait_and_add, bins)
    bins = SIDEWAYS_FACTOR * (bins[0:32] + bins[32:64])
    lateral_flow = jnp.concatenate([bins[0:16], bins[16:32]], 1)

    segments = lateral_flow.shape[0]
    offset_term = gain * lateral_flow + rest
    gains, offsets = [gain[0:1]], [offset_term[0:1]]
    for i in range(1, segments):
        g = gain[i : i + 1]
        gains.append(g * gains[-1])
        offsets.append(g * offsets[-1] + offset_term[i : i + 1])

    leave[0:1] = gains[-1]
    leave[1:2] = offsets[-1]
    leave[2:3] = outlet_ref[...].astype(jnp.float32)
    leave[3:8] = jnp.zeros((5, leave.shape[1]), jnp.float32)

    def leave_copy(d):
        return pltpu.make_async_remote_copy(
            src_ref=leave,
            dst_ref=met.at[d],
            send_sem=leave_send.at[d],
            recv_sem=leave_recv.at[d],
            device_id=(my_row + d, my_col),
            device_id_type=MESH,
        )

    for d in range(1, n_row):

        @pl.when(my_row + d < n_row)
        def _():
            leave_copy(d).start()

    edge_cols[...] = jnp.zeros_like(edge_cols)

    @pl.when(has_right)
    def _():
        col_copy(True).wait_recv()
        packed = from_right[...]
        for p in range(2 * layers):
            part = pltpu.roll(packed, 128 - SUB * p, 1) if p else packed
            edge_cols[p // layers, p % layers] = jnp.where(lane < SUB, part, 0.0)

    @pl.when(has_left)
    def _():
        col_copy(False).wait_recv()
        packed = from_left[...]
        for p in range(2 * layers):
            part = pltpu.roll(packed, 128 - SUB - SUB * p, 1)
            edge_cols[p // layers, p % layers] = jnp.where(
                lane >= 128 - SUB, part, edge_cols[p // layers, p % layers]
            )

    def lateral(l, carry):
        m = jnp.concatenate([tall(0, l, slice(0, cols)), edge_cols[0, l]], 1)
        last, edge, side = cond_ref[l, rows - 8 : rows, :], edge_rows[1, l], edge_cols[1, l]
        strip = jnp.concatenate([last, edge, cond_ref[l, 0:8, :]], 0)
        low = jnp.concatenate([faces[0, l, 0 : rows - 8, :], face(strip, 0)[0:16]], 0)
        face_down = jnp.concatenate([low, face(side, 0)], 1)
        strip = jnp.concatenate(
            [cond_ref[l, :, cols - 128 : cols], side[0:rows], cond_ref[l, :, 0:128]], 1
        )
        wide = jnp.concatenate([faces[1, l, :, 0 : cols - 128], face(strip, 1)[:, 0:256]], 1)
        face_right = jnp.concatenate([wide, face(jnp.concatenate([edge, side[rows:]], 1), 1)], 0)
        for _ in range(SUB):
            flux_down = face_down * (pltpu.roll(m, height - 1, 0) - m)
            flux_right = face_right * (pltpu.roll(m, width - 1, 1) - m)
            m = m + (
                (flux_down - pltpu.roll(flux_down, 1, 0))
                + (flux_right - pltpu.roll(flux_right, 1, 1))
            )
        moved_ref[l] = m[0:rows, 0:cols]
        return carry

    lax.fori_loop(0, layers, lateral, 0, unroll=2)

    boundary[...] = jnp.zeros_like(boundary)
    reach_lane = lax.broadcasted_iota(jnp.int32, (128, 128), 0).astype(jnp.float32)
    row16 = lax.broadcasted_iota(jnp.int32, (16, 128), 0)
    for d in range(n_row - 1, 0, -1):

        @pl.when(my_row >= d)
        def _():
            leave_copy(d).wait_recv()
            block = met[d]
            goal = jnp.where(reach_lane == block[2:3], 1.0, 0.0).astype(jnp.bfloat16)
            flow = jnp.broadcast_to(block[0:1] * boundary[0:1] + block[1:2], (16, 128))
            first = flow.astype(jnp.bfloat16).astype(jnp.float32)
            second = (flow - first).astype(jnp.bfloat16).astype(jnp.float32)
            third = flow - first - second
            pieces = jnp.where(
                row16 == 0, first, jnp.where(row16 == 1, second, jnp.where(row16 == 2, third, 0.0))
            ).astype(jnp.bfloat16)
            got = lax.dot_general(pieces, goal, NT, preferred_element_type=jnp.float32)
            boundary[0:1] = got[0:1] + got[1:2] + got[2:3]

    enter = boundary[0:1]
    flows = [gains[i] * enter + offsets[i] for i in range(segments)]
    flow_ref[...] = jnp.concatenate(flows, 0)
    inflow_ref[...] = jnp.concatenate([enter] + flows[:-1], 0) + lateral_flow

    lists_wait(send_sem, 1, devices - 1)

    @pl.when(has_up)
    def _():
        row_copy(True).wait_send()

    @pl.when(has_down)
    def _():
        row_copy(False).wait_send()

    @pl.when(has_left)
    def _():
        col_copy(True).wait_send()

    @pl.when(has_right)
    def _():
        col_copy(False).wait_send()

    for d in range(1, n_row):

        @pl.when(my_row + d < n_row)
        def _():
            leave_copy(d).wait_send()


def exchange_step(moisture, lateral_cond, sent, reach, travel, out_b, in_b, outlet):
    layers, rows, cols = moisture.shape
    devices = sent.shape[0]
    n_row = lax.axis_size("row")
    height = rows + 8
    f32 = jnp.float32
    vmem = pl.BlockSpec(memory_space=pltpu.VMEM)
    dma = pltpu.SemaphoreType.DMA
    return pl.pallas_call(
        step_kernel,
        in_specs=[vmem] * 8,
        out_specs=[vmem] * 3,
        out_shape=[
            jax.ShapeDtypeStruct(moisture.shape, f32),
            jax.ShapeDtypeStruct(travel.shape, f32),
            jax.ShapeDtypeStruct(travel.shape, f32),
        ],
        scratch_shapes=[
            pltpu.VMEM((2, layers, 8, cols), f32),
            pltpu.VMEM((2, layers, height, 128), f32),
            pltpu.VMEM((layers, 8, cols), f32),
            pltpu.VMEM((layers, 8, cols), f32),
            pltpu.VMEM((layers, 8, cols), f32),
            pltpu.VMEM((layers, 8, cols), f32),
            pltpu.VMEM((height, 128), f32),
            pltpu.VMEM((height, 128), f32),
            pltpu.VMEM((height, 128), f32),
            pltpu.VMEM((height, 128), f32),
            pltpu.VMEM((devices, 8, 128), f32),
            pltpu.VMEM((2, layers, rows, cols), f32),
            pltpu.VMEM((8, 128), f32),
            pltpu.VMEM((n_row, 8, 128), f32),
            pltpu.VMEM((8, 128), f32),
            dma,
            dma((n_row,)),
            dma((2,)),
            dma((2,)),
            dma((2,)),
            dma((2,)),
            dma,
            dma((n_row,)),
            dma((n_row,)),
        ],
        compiler_params=pltpu.CompilerParams(
            collective_id=0, has_side_effects=True, vmem_limit_bytes=24 * 1024 * 1024
        ),
        name="exchange_step",
    )(moisture, lateral_cond, sent, reach, travel, out_b, in_b, outlet)


def finish_kernel(
    moved_ref, vert_ref, rain_ref, moist_ref, flow_in_ref, inflow_in_ref,
    new_ref, flow_ref, inflow_ref,
    solved, new_sem, flow_sem,
):
    layers, rows, _ = moved_ref.shape
    steps = rows // 8
    flow_copies = [
        pltpu.make_async_copy(flow_in_ref, flow_ref, flow_sem.at[0]),
        pltpu.make_async_copy(inflow_in_ref, inflow_ref, flow_sem.at[1]),
    ]
    for copy in flow_copies:
        copy.start()

    def new_copy(i):
        at = pl.ds(pl.multiple_of(i * 8, 8), 8)
        return pltpu.make_async_copy(solved.at[:, at, :], new_ref.at[:, at, :], new_sem.at[i])

    def solve(i, carry):
        at = pl.ds(pl.multiple_of(i * 8, 8), 8)
        upper, value = [], []
        for l in range(layers):
            v = vert_ref[l, at, :]
            right = moved_ref[l, at, :]
            if l == 0:
                wet = moist_ref[0, at, :]
                right = right + (rain_ref[at, :] - rain_ref[at, :] * (4.0 * wet * wet))
                diag = 1.0 + v
            else:
                diag = 1.0 + v + above * (1.0 - upper[-1])
                right = right + above * value[-1]
            inverse = 1.0 / diag
            upper.append(v * inverse)
            value.append(right * inverse)
            above = v
        x = value[-1]
        solved[layers - 1, at, :] = x
        for l in range(layers - 2, -1, -1):
            x = value[l] + upper[l] * x
            solved[l, at, :] = x
        new_copy(i).start()
        return carry

    lax.fori_loop(0, steps, solve, 0, unroll=2)
    for copy in flow_copies:
        copy.wait()
    for i in range(steps):
        new_copy(i).wait()


def finish(moved, vertical_cond, rain, moisture, flow, inflow):
    vmem = pl.BlockSpec(memory_space=pltpu.VMEM)
    out = pl.BlockSpec(memory_space=pl.ANY)
    return pl.pallas_call(
        finish_kernel,
        in_specs=[vmem] * 6,
        out_specs=[out] * 3,
        out_shape=[
            jax.ShapeDtypeStruct(moved.shape, jnp.float32),
            jax.ShapeDtypeStruct(flow.shape, jnp.float32),
            jax.ShapeDtypeStruct(flow.shape, jnp.float32),
        ],
        scratch_shapes=[
            pltpu.VMEM(moved.shape, jnp.float32),
            pltpu.SemaphoreType.DMA((moved.shape[1] // 8,)),
            pltpu.SemaphoreType.DMA((2,)),
        ],
        compiler_params=pltpu.CompilerParams(vmem_limit_bytes=16 * 1024 * 1024),
        name="finish",
    )(moved, vertical_cond, rain, moisture, flow, inflow)


def shards(
    moisture,
    lateral_cond,
    vertical_cond,
    rain,
    remap_cell,
    remap_reach,
    travel_time,
    outflow_before,
    inflow_before,
    outlet_lane,
):
    sent = look_up(moisture, vertical_cond, rain, remap_cell)
    reach = remap_reach.reshape(sent.shape)
    moved, flow, inflow = exchange_step(
        moisture, lateral_cond, sent, reach, travel_time, outflow_before, inflow_before, outlet_lane
    )
    return tuple(finish(moved, vertical_cond, rain, moisture, flow, inflow))


def solution(mesh):
    in_specs = (
        P(None, "row", "col"),
        P(None, "row", "col"),
        P(None, "row", "col"),
        P("row", "col"),
        P(("row", "col"), None, None),
        P(None, ("row", "col"), None),
        P("row", "col"),
        P("row", "col"),
        P("row", "col"),
        P("row", "col"),
    )
    out_specs = (P(None, "row", "col"), P("row", "col"), P("row", "col"))
    return jax.shard_map(shards, mesh=mesh, in_specs=in_specs, out_specs=out_specs, check_vma=False)
```

```python
import functools
import math

import jax
import jax.numpy as jnp
from jax import lax
from jax.experimental import pallas as pl
from jax.experimental.pallas import tpu as pltpu
from jax.sharding import PartitionSpec as P

SUB = 3
WEIGHT_X = 0.2
SIDEWAYS_FACTOR = 0.01

RUNOFF_LOW = 0.0025
RUNOFF_HIGH = 1.31
LOG_LOW = math.log(RUNOFF_LOW)
CODE_MAX = 65535.0
LOG_STEP = (math.log(RUNOFF_HIGH) - LOG_LOW) / CODE_MAX

BY_MATRIX = 4
UNROLL = 8
MESH = pl.DeviceIdType.MESH
NT = (((1,), (1,)), ((), ()))


def lookup_kernel(
    moist_ref, vert_ref, rain_ref, cell_ref, out_ref,
    fields, cells, table, pieces, stage, looked, counts_vec, counts, chunks, sem, fetch_sem,
):
    dests, per = cells.shape[0:2]
    last = moist_ref.shape[0] - 1
    parts = [moist_ref.at[0], moist_ref.at[last], vert_ref.at[last], rain_ref]
    field_fetches = [
        pltpu.make_async_copy(part, fields.at[i], fetch_sem.at[per + i])
        for i, part in enumerate(parts)
    ]
    for fetch in field_fetches:
        fetch.start()
    fetches = [
        pltpu.make_async_copy(
            cell_ref.at[0, :, j * 128 : (j + 1) * 128], cells.at[:, j, :], fetch_sem.at[j]
        )
        for j in range(per)
    ]
    for fetch in fetches:
        fetch.start()

    for fetch in field_fetches:
        fetch.wait()
    runoff = fields[3] * (4.0 * fields[0] * fields[0]) + fields[2] * fields[1]
    code = (jnp.log(runoff) - LOG_LOW) * (1.0 / LOG_STEP)
    code = jnp.clip(jnp.round(code), 0.0, CODE_MAX).astype(jnp.int32)
    rows = runoff.shape[0]
    for k in range(2):
        low = code[:, k * 128 : (k + 1) * 128]
        high = code[:, (k + 2) * 128 : (k + 3) * 128]
        table[k * rows : (k + 1) * rows, :] = low | (high << 16)

    turned = jnp.transpose(
        jnp.concatenate([runoff[:, k * 128 : (k + 1) * 128] for k in range(4)], 0)
    )
    first = turned.astype(jnp.bfloat16)
    pieces[0:128, :] = first
    pieces[128:256, :] = (turned - first.astype(jnp.float32)).astype(jnp.bfloat16)

    out_ref[...] = jnp.zeros_like(out_ref)
    sub = lax.broadcasted_iota(jnp.int32, (8, 128), 0)
    sub16 = lax.broadcasted_iota(jnp.int32, (16, 128), 0).astype(jnp.float32).astype(jnp.bfloat16)
    zero = jnp.zeros((16, 128), jnp.bfloat16)
    one = jnp.ones((16, 128), jnp.bfloat16)

    def row_hits(table_row, s):
        wanted = jnp.broadcast_to(table_row[s : s + 1], (16, 128)).astype(jnp.bfloat16)
        return jnp.concatenate(
            [jnp.where(sub16 + jnp.bfloat16(16 * t) == wanted, one, zero) for t in range(16)], 0
        )

    def pick_lane(found, lane):
        bits = [((lane >> b) & 1) == 1 for b in range(3, 7)]
        total = None
        for p in range(2):
            level = [found[128 * p + 8 * t : 128 * p + 8 * t + 8] for t in range(16)]
            for bit in bits:
                level = [
                    jnp.where(bit, level[2 * t + 1], level[2 * t]) for t in range(len(level) // 2)
                ]
            total = level[0] if total is None else total + level[0]
        return jnp.sum(jnp.where(sub == (lane & 7), total, 0.0), axis=0, keepdims=True)

    for fetch in fetches:
        fetch.wait()
    live = jnp.sum(jnp.where(cells[...] >= 0, 1, 0), axis=1)
    counts_vec[...] = jnp.transpose(live)[0:8, :]
    copy = pltpu.make_async_copy(counts_vec, counts, sem)
    copy.start()
    copy.wait()

    def enlist(d, total):
        for j in range(per):
            chunks[total + j] = d * per + j
        return total + counts[0, d]

    total = lax.fori_loop(0, dests, enlist, jnp.int32(0), unroll=8)
    for i in range(8 * UNROLL):
        chunks[total + i] = 0

    def look_up_from(begin, vectors, by_matrix):
        for u in range(vectors):
            for s in range(8):
                e = chunks[begin + u * 8 + s]
                stage[u, s : s + 1, :] = cells[e >> 3, pl.ds(e & 7, 1), :]
        found = []
        for u in range(vectors - by_matrix, vectors):
            cell = stage[u]
            table_row = (((cell >> 9) & 63) | ((cell >> 1) & 192)).astype(jnp.float32)
            for s in range(0, 8, 2):
                hits = jnp.concatenate([row_hits(table_row, s), row_hits(table_row, s + 1)], 1)
                found.append(jnp.dot(pieces[...], hits, preferred_element_type=jnp.float32))
        for u in range(vectors - by_matrix):
            cell = stage[u]
            lane = cell & 127
            word_row = ((cell >> 9) & 63) | ((cell >> 1) & 64)
            odd = [None, None]
            for t in range(2 * rows):
                row = jnp.broadcast_to(table[t : t + 1, :], (8, 128))
                got = jnp.take_along_axis(row, lane, axis=1, mode="promise_in_bounds")
                old = odd[t % 2]
                odd[t % 2] = got if old is None else jnp.where(word_row == t, got, old)
            word = jnp.where((word_row & 1) == 1, odd[1], odd[0])
            half = jnp.where(((cell >> 8) & 1) == 1, word >> 16, word) & 65535
            value = jnp.exp(half.astype(jnp.float32) * LOG_STEP + LOG_LOW)
            looked[u] = jnp.where(cell >= 0, value, 0.0)
        for u in range(vectors - by_matrix, vectors):
            cell = stage[u]
            for s in range(8):
                both = found[(u - vectors + by_matrix) * 4 + s // 2]
                lane = jnp.broadcast_to(cell[s : s + 1] & 127, (8, 128))
                value = pick_lane(both[:, (s % 2) * 128 : (s % 2 + 1) * 128], lane)
                looked[u, s : s + 1, :] = jnp.where(cell[s : s + 1] >= 0, value, 0.0)
        for u in range(vectors):
            for s in range(8):
                e = chunks[begin + u * 8 + s]
                out_ref[e >> 3, pl.ds(e & 7, 1), :] = looked[u, s : s + 1, :]

    whole = total // (8 * UNROLL)
    left = total - whole * (8 * UNROLL)

    @pl.loop(0, whole)
    def _(g):
        look_up_from(g * (8 * UNROLL), UNROLL, BY_MATRIX)

    @pl.loop(0, (left + (4 * UNROLL - 1)) // (4 * UNROLL))
    def _(g):
        look_up_from(whole * (8 * UNROLL) + g * (4 * UNROLL), UNROLL // 2, BY_MATRIX // 2)


def look_up(moisture, vertical_cond, rain, remap_cell):
    layers, rows, cols = moisture.shape
    dests, slots = remap_cell.shape[1:]
    return pl.pallas_call(
        lookup_kernel,
        in_specs=[pl.BlockSpec(memory_space=pltpu.HBM)] * 4,
        out_specs=pl.BlockSpec(memory_space=pltpu.VMEM),
        out_shape=jax.ShapeDtypeStruct((dests, slots // 128, 128), jnp.float32),
        scratch_shapes=[
            pltpu.VMEM((4, rows, cols), jnp.float32),
            pltpu.VMEM((dests, slots // 128, 128), jnp.int32),
            pltpu.VMEM((2 * rows, 128), jnp.int32),
            pltpu.VMEM((256, 4 * rows), jnp.bfloat16),
            pltpu.VMEM((UNROLL, 8, 128), jnp.int32),
            pltpu.VMEM((UNROLL, 8, 128), jnp.float32),
            pltpu.VMEM((8, dests), jnp.int32),
            pltpu.SMEM((8, dests), jnp.int32),
            pltpu.SMEM((dests * (slots // 128) + 8 * UNROLL + 8,), jnp.int32),
            pltpu.SemaphoreType.DMA,
            pltpu.SemaphoreType.DMA((slots // 128 + 4,)),
        ],
        compiler_params=pltpu.CompilerParams(vmem_limit_bytes=53 * 1024 * 1024),
        name="look_up",
    )(moisture, vertical_cond, rain, remap_cell)


HALF_BINS = 64


def step_kernel(
    moist_ref, cond_ref, sent_ref, reach_ref,
    travel_ref, out_before_ref, in_before_ref, outlet_ref,
    moved_ref, flow_ref, inflow_ref,
    edge_rows, edge_cols, pack_up, pack_down, below, above, pack_left, pack_right, from_right, from_left,
    arrived, faces, leave, met, boundary,
    send_sem, recv_sem, row_send, row_recv, col_send, col_recv, own_sem, leave_send, leave_recv,
):
    n_row, n_col = lax.axis_size("row"), lax.axis_size("col")
    devices = n_row * n_col
    my_row, my_col = lax.axis_index("row"), lax.axis_index("col")
    me = my_row * n_col + my_col
    layers, rows, cols = moist_ref.shape
    height, width = rows + 8, cols + 128
    fields = (moist_ref, cond_ref)

    barrier = pltpu.get_barrier_semaphore()

    def wrap(x, size):
        return jnp.where(x >= size, x - size, x)

    ahead = [wrap(my_col + dc, n_col) for dc in range(n_col)]
    behind = [wrap(my_col + n_col - dc, n_col) for dc in range(n_col)]

    def greet(dr, first):
        row = wrap(my_row + dr, n_row)
        for dc in range(first, n_col):
            pl.semaphore_signal(
                barrier, inc=1, device_id=(row, ahead[dc]), device_id_type=MESH
            )

    greet(0, 1)

    @pl.loop(1, n_row)
    def _(dr):
        greet(dr, 0)

    travel = travel_ref[...]
    denom = 1.0 / (1.0 + 2.0 * travel * (1.0 - WEIGHT_X))
    gain = (1.0 - 2.0 * travel * WEIGHT_X) * denom
    rest = (1.0 + 2.0 * travel * WEIGHT_X) * denom * in_before_ref[...]
    rest += (2.0 * travel * (1.0 - WEIGHT_X) - 1.0) * denom * out_before_ref[...]

    has_up, has_down = my_row > 0, my_row < n_row - 1
    has_left, has_right = my_col > 0, my_col < n_col - 1

    sub = lax.broadcasted_iota(jnp.int32, (layers, 8, cols), 1)
    pack_up[...] = jnp.where(
        sub < SUB, moist_ref[:, 0:8, :], pltpu.roll(cond_ref[:, 0:8, :], 8 - SUB, 1)
    )
    pack_down[...] = jnp.where(
        sub >= 8 - SUB,
        moist_ref[:, rows - 8 : rows, :],
        pltpu.roll(cond_ref[:, rows - 8 : rows, :], SUB, 1),
    )

    def row_copy(up):
        return pltpu.make_async_remote_copy(
            src_ref=pack_up if up else pack_down,
            dst_ref=below if up else above,
            send_sem=row_send.at[0 if up else 1],
            recv_sem=row_recv.at[0 if up else 1],
            device_id=(my_row - 1 if up else my_row + 1, my_col),
            device_id_type=MESH,
        )

    pl.semaphore_wait(barrier, devices - 1)

    def send_lists(dr, first):
        row = wrap(my_row + dr, n_row)
        for dc in range(first, n_col):
            pltpu.make_async_remote_copy(
                src_ref=sent_ref.at[row * n_col + ahead[dc]],
                dst_ref=arrived.at[dr * n_col + dc],
                send_sem=send_sem,
                recv_sem=recv_sem.at[dr],
                device_id=(row, ahead[dc]),
                device_id_type=MESH,
            ).start()

    send_lists(0, 1)

    @pl.loop(1, n_row)
    def _(dr):
        send_lists(dr, 0)

    def lists_wait(sem, first, count):
        place = arrived.at[pl.ds(first, count)]
        pltpu.make_async_copy(place, place, sem).wait()

    @pl.when(has_up)
    def _():
        row_copy(True).start()

    @pl.when(has_down)
    def _():
        row_copy(False).start()

    own = pltpu.make_async_copy(sent_ref.at[me], arrived.at[0], own_sem)
    own.start()

    def face(c, axis):
        size = c.shape[axis]
        near = pltpu.roll(c, size - 1, axis)
        return 2.0 * c * near / jnp.maximum(c + near, 1e-30)

    def inner_faces(l, carry):
        c = cond_ref[l]
        faces[0, l] = face(c, 0)
        faces[1, l] = face(c, 1)
        return carry

    lax.fori_loop(0, layers, inner_faces, 0)

    own.wait()
    base = lax.broadcasted_iota(jnp.int32, (16, 1024), 0).astype(jnp.float32).astype(jnp.bfloat16)
    zero = jnp.zeros((16, 1024), jnp.bfloat16)
    one = jnp.ones((16, 1024), jnp.bfloat16)

    def spread(x):
        return jnp.concatenate(
            [jnp.broadcast_to(x[j : j + 1, :], (16, 128)).astype(jnp.bfloat16) for j in range(8)], 1
        )

    def add_up(dr, acc):
        row = wrap(my_row + n_row - dr, n_row)
        for dc in range(n_col):
            k = dr * n_col + dc
            q = reach_ref[row * n_col + behind[dc]]
            value = arrived[k]
            first = value.astype(jnp.bfloat16).astype(jnp.float32)
            head, tail = spread(first), spread(value - first)
            a = spread(((q >> 7) + 16 * ((q >> 6) & 1)).astype(jnp.float32))
            b = spread((q & 63).astype(jnp.float32))
            hits = [base + jnp.bfloat16(16 * t) == a for t in range(2)]
            values = jnp.concatenate(
                [jnp.where(h, head, zero) for h in hits] + [jnp.where(h, tail, zero) for h in hits], 0
            )
            places = jnp.concatenate(
                [jnp.where(base + jnp.bfloat16(16 * t) == b, one, zero) for t in range(4)], 0
            )
            acc = acc + lax.dot_general(values, places, NT, preferred_element_type=jnp.float32)
        return acc

    def wait_and_add(dr, acc):
        lists_wait(recv_sem.at[dr], dr * n_col, n_col)
        return add_up(dr, acc)

    lists_wait(recv_sem.at[0], 1, n_col - 1)
    bins = add_up(0, jnp.zeros((64, HALF_BINS), jnp.float32))
    bins = lax.fori_loop(1, n_row // 2, wait_and_add, bins)

    edge_rows[...] = jnp.zeros_like(edge_rows)

    @pl.when(has_down)
    def _():
        row_copy(True).wait_recv()
        edge_rows[0] = jnp.where(sub < SUB, below[...], 0.0)
        edge_rows[1] = jnp.where(sub < SUB, pltpu.roll(below[...], SUB, 1), 0.0)

    @pl.when(has_up)
    def _():
        row_copy(False).wait_recv()
        edge_rows[0] = jnp.where(sub >= 8 - SUB, above[...], edge_rows[0])
        edge_rows[1] = jnp.where(sub >= 8 - SUB, pltpu.roll(above[...], 8 - SUB, 1), edge_rows[1])

    def tall(f, l, lanes):
        return jnp.concatenate([fields[f][l, :, lanes], edge_rows[f, l, :, lanes]], 0)

    lane = lax.broadcasted_iota(jnp.int32, (height, 128), 1)
    left_pack = jnp.zeros((height, 128), jnp.float32)
    right_pack = jnp.zeros((height, 128), jnp.float32)
    for p in range(2 * layers):
        here = (lane >= SUB * p) & (lane < SUB * (p + 1))
        first = tall(p // layers, p % layers, slice(0, 128))
        last = tall(p // layers, p % layers, slice(cols - 128, cols))
        left_pack = jnp.where(here, pltpu.roll(first, SUB * p, 1) if p else first, left_pack)
        right_pack = jnp.where(here, pltpu.roll(last, SUB * p + SUB, 1), right_pack)
    pack_left[...] = left_pack
    pack_right[...] = right_pack

    def col_copy(left):
        return pltpu.make_async_remote_copy(
            src_ref=pack_left if left else pack_right,
            dst_ref=from_right if left else from_left,
            send_sem=col_send.at[0 if left else 1],
            recv_sem=col_recv.at[0 if left else 1],
            device_id=(my_row, my_col - 1 if left else my_col + 1),
            device_id_type=MESH,
        )

    @pl.when(has_left)
    def _():
        col_copy(True).start()

    @pl.when(has_right)
    def _():
        col_copy(False).start()

    bins = lax.fori_loop(n_row // 2, n_row, wait_and_add, bins)
    bins = SIDEWAYS_FACTOR * (bins[0:32] + bins[32:64])
    lateral_flow = jnp.concatenate([bins[0:16], bins[16:32]], 1)

    segments = lateral_flow.shape[0]
    offset_term = gain * lateral_flow + rest
    gains, offsets = [gain[0:1]], [offset_term[0:1]]
    for i in range(1, segments):
        g = gain[i : i + 1]
        gains.append(g * gains[-1])
        offsets.append(g * offsets[-1] + offset_term[i : i + 1])

    leave[0:1] = gains[-1]
    leave[1:2] = offsets[-1]
    leave[2:3] = outlet_ref[...].astype(jnp.float32)
    leave[3:8] = jnp.zeros((5, leave.shape[1]), jnp.float32)

    def leave_copy(d):
        return pltpu.make_async_remote_copy(
            src_ref=leave,
            dst_ref=met.at[d],
            send_sem=leave_send.at[d],
            recv_sem=leave_recv.at[d],
            device_id=(my_row + d, my_col),
            device_id_type=MESH,
        )

    for d in range(1, n_row):

        @pl.when(my_row + d < n_row)
        def _():
            leave_copy(d).start()

    edge_cols[...] = jnp.zeros_like(edge_cols)

    @pl.when(has_right)
    def _():
        col_copy(True).wait_recv()
        packed = from_right[...]
        for p in range(2 * layers):
            part = pltpu.roll(packed, 128 - SUB * p, 1) if p else packed
            edge_cols[p // layers, p % layers] = jnp.where(lane < SUB, part, 0.0)

    @pl.when(has_left)
    def _():
        col_copy(False).wait_recv()
        packed = from_left[...]
        for p in range(2 * layers):
            part = pltpu.roll(packed, 128 - SUB - SUB * p, 1)
            edge_cols[p // layers, p % layers] = jnp.where(
                lane >= 128 - SUB, part, edge_cols[p // layers, p % layers]
            )

    def lateral(l, carry):
        m = jnp.concatenate([tall(0, l, slice(0, cols)), edge_cols[0, l]], 1)
        last, edge, side = cond_ref[l, rows - 8 : rows, :], edge_rows[1, l], edge_cols[1, l]
        strip = jnp.concatenate([last, edge, cond_ref[l, 0:8, :]], 0)
        low = jnp.concatenate([faces[0, l, 0 : rows - 8, :], face(strip, 0)[0:16]], 0)
        face_down = jnp.concatenate([low, face(side, 0)], 1)
        strip = jnp.concatenate(
            [cond_ref[l, :, cols - 128 : cols], side[0:rows], cond_ref[l, :, 0:128]], 1
        )
        wide = jnp.concatenate([faces[1, l, :, 0 : cols - 128], face(strip, 1)[:, 0:256]], 1)
        face_right = jnp.concatenate([wide, face(jnp.concatenate([edge, side[rows:]], 1), 1)], 0)
        for _ in range(SUB):
            flux_down = face_down * (pltpu.roll(m, height - 1, 0) - m)
            flux_right = face_right * (pltpu.roll(m, width - 1, 1) - m)
            m = m + (
                (flux_down - pltpu.roll(flux_down, 1, 0))
                + (flux_right - pltpu.roll(flux_right, 1, 1))
            )
        moved_ref[l] = m[0:rows, 0:cols]
        return carry

    lax.fori_loop(0, layers, lateral, 0, unroll=2)

    boundary[...] = jnp.zeros_like(boundary)
    reach_lane = lax.broadcasted_iota(jnp.int32, (128, 128), 0).astype(jnp.float32)
    row16 = lax.broadcasted_iota(jnp.int32, (16, 128), 0)
    for d in range(n_row - 1, 0, -1):

        @pl.when(my_row >= d)
        def _():
            leave_copy(d).wait_recv()
            block = met[d]
            goal = jnp.where(reach_lane == block[2:3], 1.0, 0.0).astype(jnp.bfloat16)
            flow = jnp.broadcast_to(block[0:1] * boundary[0:1] + block[1:2], (16, 128))
            first = flow.astype(jnp.bfloat16).astype(jnp.float32)
            second = (flow - first).astype(jnp.bfloat16).astype(jnp.float32)
            third = flow - first - second
            pieces = jnp.where(
                row16 == 0, first, jnp.where(row16 == 1, second, jnp.where(row16 == 2, third, 0.0))
            ).astype(jnp.bfloat16)
            got = lax.dot_general(pieces, goal, NT, preferred_element_type=jnp.float32)
            boundary[0:1] = got[0:1] + got[1:2] + got[2:3]

    enter = boundary[0:1]
    flows = [gains[i] * enter + offsets[i] for i in range(segments)]
    flow_ref[...] = jnp.concatenate(flows, 0)
    inflow_ref[...] = jnp.concatenate([enter] + flows[:-1], 0) + lateral_flow

    lists_wait(send_sem, 1, devices - 1)

    @pl.when(has_up)
    def _():
        row_copy(True).wait_send()

    @pl.when(has_down)
    def _():
        row_copy(False).wait_send()

    @pl.when(has_left)
    def _():
        col_copy(True).wait_send()

    @pl.when(has_right)
    def _():
        col_copy(False).wait_send()

    for d in range(1, n_row):

        @pl.when(my_row + d < n_row)
        def _():
            leave_copy(d).wait_send()


def exchange_step(moisture, lateral_cond, sent, reach, travel, out_b, in_b, outlet):
    layers, rows, cols = moisture.shape
    devices = sent.shape[0]
    n_row = lax.axis_size("row")
    height = rows + 8
    f32 = jnp.float32
    vmem = pl.BlockSpec(memory_space=pltpu.VMEM)
    dma = pltpu.SemaphoreType.DMA
    return pl.pallas_call(
        step_kernel,
        in_specs=[vmem] * 8,
        out_specs=[vmem] * 3,
        out_shape=[
            jax.ShapeDtypeStruct(moisture.shape, f32),
            jax.ShapeDtypeStruct(travel.shape, f32),
            jax.ShapeDtypeStruct(travel.shape, f32),
        ],
        scratch_shapes=[
            pltpu.VMEM((2, layers, 8, cols), f32),
            pltpu.VMEM((2, layers, height, 128), f32),
            pltpu.VMEM((layers, 8, cols), f32),
            pltpu.VMEM((layers, 8, cols), f32),
            pltpu.VMEM((layers, 8, cols), f32),
            pltpu.VMEM((layers, 8, cols), f32),
            pltpu.VMEM((height, 128), f32),
            pltpu.VMEM((height, 128), f32),
            pltpu.VMEM((height, 128), f32),
            pltpu.VMEM((height, 128), f32),
            pltpu.VMEM((devices, 8, 128), f32),
            pltpu.VMEM((2, layers, rows, cols), f32),
            pltpu.VMEM((8, 128), f32),
            pltpu.VMEM((n_row, 8, 128), f32),
            pltpu.VMEM((8, 128), f32),
            dma,
            dma((n_row,)),
            dma((2,)),
            dma((2,)),
            dma((2,)),
            dma((2,)),
            dma,
            dma((n_row,)),
            dma((n_row,)),
        ],
        compiler_params=pltpu.CompilerParams(
            collective_id=0, has_side_effects=True, vmem_limit_bytes=24 * 1024 * 1024
        ),
        name="exchange_step",
    )(moisture, lateral_cond, sent, reach, travel, out_b, in_b, outlet)


def finish_kernel(
    moved_ref, vert_ref, rain_ref, moist_ref, flow_in_ref, inflow_in_ref,
    new_ref, flow_ref, inflow_ref,
    solved, new_sem, flow_sem,
):
    layers, rows, _ = moved_ref.shape
    steps = rows // 8
    flow_copies = [
        pltpu.make_async_copy(flow_in_ref, flow_ref, flow_sem.at[0]),
        pltpu.make_async_copy(inflow_in_ref, inflow_ref, flow_sem.at[1]),
    ]
    for copy in flow_copies:
        copy.start()

    def new_copy(i):
        at = pl.ds(pl.multiple_of(i * 8, 8), 8)
        return pltpu.make_async_copy(solved.at[:, at, :], new_ref.at[:, at, :], new_sem.at[i])

    def solve(i, carry):
        at = pl.ds(pl.multiple_of(i * 8, 8), 8)
        upper, value = [], []
        for l in range(layers):
            v = vert_ref[l, at, :]
            right = moved_ref[l, at, :]
            if l == 0:
                wet = moist_ref[0, at, :]
                right = right + (rain_ref[at, :] - rain_ref[at, :] * (4.0 * wet * wet))
                diag = 1.0 + v
            else:
                diag = 1.0 + v + above * (1.0 - upper[-1])
                right = right + above * value[-1]
            inverse = 1.0 / diag
            upper.append(v * inverse)
            value.append(right * inverse)
            above = v
        x = value[-1]
        solved[layers - 1, at, :] = x
        for l in range(layers - 2, -1, -1):
            x = value[l] + upper[l] * x
            solved[l, at, :] = x
        new_copy(i).start()
        return carry

    lax.fori_loop(0, steps, solve, 0, unroll=2)
    for copy in flow_copies:
        copy.wait()
    for i in range(steps):
        new_copy(i).wait()


def finish(moved, vertical_cond, rain, moisture, flow, inflow):
    vmem = pl.BlockSpec(memory_space=pltpu.VMEM)
    out = pl.BlockSpec(memory_space=pl.ANY)
    return pl.pallas_call(
        finish_kernel,
        in_specs=[vmem] * 6,
        out_specs=[out] * 3,
        out_shape=[
            jax.ShapeDtypeStruct(moved.shape, jnp.float32),
            jax.ShapeDtypeStruct(flow.shape, jnp.float32),
            jax.ShapeDtypeStruct(flow.shape, jnp.float32),
        ],
        scratch_shapes=[
            pltpu.VMEM(moved.shape, jnp.float32),
            pltpu.SemaphoreType.DMA((moved.shape[1] // 8,)),
            pltpu.SemaphoreType.DMA((2,)),
        ],
        compiler_params=pltpu.CompilerParams(vmem_limit_bytes=16 * 1024 * 1024),
        name="finish",
    )(moved, vertical_cond, rain, moisture, flow, inflow)


def shards(
    moisture,
    lateral_cond,
    vertical_cond,
    rain,
    remap_cell,
    remap_reach,
    travel_time,
    outflow_before,
    inflow_before,
    outlet_lane,
):
    sent = look_up(moisture, vertical_cond, rain, remap_cell)
    reach = remap_reach.reshape(sent.shape)
    moved, flow, inflow = exchange_step(
        moisture, lateral_cond, sent, reach, travel_time, outflow_before, inflow_before, outlet_lane
    )
    return tuple(finish(moved, vertical_cond, rain, moisture, flow, inflow))


def solution(mesh):
    in_specs = (
        P(None, "row", "col"),
        P(None, "row", "col"),
        P(None, "row", "col"),
        P("row", "col"),
        P(("row", "col"), None, None),
        P(None, ("row", "col"), None),
        P("row", "col"),
        P("row", "col"),
        P("row", "col"),
        P("row", "col"),
    )
    out_specs = (P(None, "row", "col"), P("row", "col"), P("row", "col"))
    return jax.shard_map(shards, mesh=mesh, in_specs=in_specs, out_specs=out_specs, check_vma=False)
```

```python
import functools
import math

import jax
import jax.numpy as jnp
from jax import lax
from jax.experimental import pallas as pl
from jax.experimental.pallas import tpu as pltpu
from jax.sharding import PartitionSpec as P

SUB = 3
WEIGHT_X = 0.2
SIDEWAYS_FACTOR = 0.01

RUNOFF_LOW = 0.0025
RUNOFF_HIGH = 1.31
LOG_LOW = math.log(RUNOFF_LOW)
CODE_MAX = 65535.0
LOG_STEP = (math.log(RUNOFF_HIGH) - LOG_LOW) / CODE_MAX

BY_MATRIX = 5
UNROLL = 10
MESH = pl.DeviceIdType.MESH
NT = (((1,), (1,)), ((), ()))


def lookup_kernel(
    moist_ref, vert_ref, rain_ref, cell_ref, out_ref,
    fields, cells, table, pieces, stage, looked, counts_vec, counts, chunks, sem, fetch_sem,
):
    dests, per = cells.shape[0:2]
    last = moist_ref.shape[0] - 1
    parts = [moist_ref.at[0], moist_ref.at[last], vert_ref.at[last], rain_ref]
    field_fetches = [
        pltpu.make_async_copy(part, fields.at[i], fetch_sem.at[per + i])
        for i, part in enumerate(parts)
    ]
    for fetch in field_fetches:
        fetch.start()
    fetches = [
        pltpu.make_async_copy(
            cell_ref.at[0, :, j * 128 : (j + 1) * 128], cells.at[:, j, :], fetch_sem.at[j]
        )
        for j in range(per)
    ]
    for fetch in fetches:
        fetch.start()

    for fetch in field_fetches:
        fetch.wait()
    runoff = fields[3] * (4.0 * fields[0] * fields[0]) + fields[2] * fields[1]
    code = (jnp.log(runoff) - LOG_LOW) * (1.0 / LOG_STEP)
    code = jnp.clip(jnp.round(code), 0.0, CODE_MAX).astype(jnp.int32)
    rows = runoff.shape[0]
    for k in range(2):
        low = code[:, k * 128 : (k + 1) * 128]
        high = code[:, (k + 2) * 128 : (k + 3) * 128]
        table[k * rows : (k + 1) * rows, :] = low | (high << 16)

    turned = jnp.transpose(
        jnp.concatenate([runoff[:, k * 128 : (k + 1) * 128] for k in range(4)], 0)
    )
    first = turned.astype(jnp.bfloat16)
    pieces[0:128, :] = first
    pieces[128:256, :] = (turned - first.astype(jnp.float32)).astype(jnp.bfloat16)

    out_ref[...] = jnp.zeros_like(out_ref)
    sub = lax.broadcasted_iota(jnp.int32, (8, 128), 0)
    sub16 = lax.broadcasted_iota(jnp.int32, (16, 128), 0).astype(jnp.float32).astype(jnp.bfloat16)
    zero = jnp.zeros((16, 128), jnp.bfloat16)
    one = jnp.ones((16, 128), jnp.bfloat16)

    def row_hits(table_row, s):
        wanted = jnp.broadcast_to(table_row[s : s + 1], (16, 128)).astype(jnp.bfloat16)
        return jnp.concatenate(
            [jnp.where(sub16 + jnp.bfloat16(16 * t) == wanted, one, zero) for t in range(16)], 0
        )

    def pick_lane(found, lane):
        bits = [((lane >> b) & 1) == 1 for b in range(3, 7)]
        total = None
        for p in range(2):
            level = [found[128 * p + 8 * t : 128 * p + 8 * t + 8] for t in range(16)]
            for bit in bits:
                level = [
                    jnp.where(bit, level[2 * t + 1], level[2 * t]) for t in range(len(level) // 2)
                ]
            total = level[0] if total is None else total + level[0]
        return jnp.sum(jnp.where(sub == (lane & 7), total, 0.0), axis=0, keepdims=True)

    for fetch in fetches:
        fetch.wait()
    live = jnp.sum(jnp.where(cells[...] >= 0, 1, 0), axis=1)
    counts_vec[...] = jnp.transpose(live)[0:8, :]
    copy = pltpu.make_async_copy(counts_vec, counts, sem)
    copy.start()
    copy.wait()

    def enlist(d, total):
        for j in range(per):
            chunks[total + j] = d * per + j
        return total + counts[0, d]

    total = lax.fori_loop(0, dests, enlist, jnp.int32(0), unroll=8)
    for i in range(8 * UNROLL):
        chunks[total + i] = 0

    def look_up_from(begin, vectors, by_matrix):
        for u in range(vectors):
            for s in range(8):
                e = chunks[begin + u * 8 + s]
                stage[u, s : s + 1, :] = cells[e >> 3, pl.ds(e & 7, 1), :]
        found = []
        for u in range(vectors - by_matrix, vectors):
            cell = stage[u]
            table_row = (((cell >> 9) & 63) | ((cell >> 1) & 192)).astype(jnp.float32)
            for s in range(0, 8, 2):
                hits = jnp.concatenate([row_hits(table_row, s), row_hits(table_row, s + 1)], 1)
                found.append(jnp.dot(pieces[...], hits, preferred_element_type=jnp.float32))
        for u in range(vectors - by_matrix):
            cell = stage[u]
            lane = cell & 127
            word_row = ((cell >> 9) & 63) | ((cell >> 1) & 64)
            odd = [None, None]
            for t in range(2 * rows):
                row = jnp.broadcast_to(table[t : t + 1, :], (8, 128))
                got = jnp.take_along_axis(row, lane, axis=1, mode="promise_in_bounds")
                old = odd[t % 2]
                odd[t % 2] = got if old is None else jnp.where(word_row == t, got, old)
            word = jnp.where((word_row & 1) == 1, odd[1], odd[0])
            half = jnp.where(((cell >> 8) & 1) == 1, word >> 16, word) & 65535
            value = jnp.exp(half.astype(jnp.float32) * LOG_STEP + LOG_LOW)
            looked[u] = jnp.where(cell >= 0, value, 0.0)
        for u in range(vectors - by_matrix, vectors):
            cell = stage[u]
            for s in range(8):
                both = found[(u - vectors + by_matrix) * 4 + s // 2]
                lane = jnp.broadcast_to(cell[s : s + 1] & 127, (8, 128))
                value = pick_lane(both[:, (s % 2) * 128 : (s % 2 + 1) * 128], lane)
                looked[u, s : s + 1, :] = jnp.where(cell[s : s + 1] >= 0, value, 0.0)
        for u in range(vectors):
            for s in range(8):
                e = chunks[begin + u * 8 + s]
                out_ref[e >> 3, pl.ds(e & 7, 1), :] = looked[u, s : s + 1, :]

    whole = total // (8 * UNROLL)
    left = total - whole * (8 * UNROLL)

    @pl.loop(0, whole)
    def _(g):
        look_up_from(g * (8 * UNROLL), UNROLL, BY_MATRIX)

    @pl.loop(0, (left + (4 * UNROLL - 1)) // (4 * UNROLL))
    def _(g):
        look_up_from(whole * (8 * UNROLL) + g * (4 * UNROLL), UNROLL // 2, BY_MATRIX // 2)


def look_up(moisture, vertical_cond, rain, remap_cell):
    layers, rows, cols = moisture.shape
    dests, slots = remap_cell.shape[1:]
    return pl.pallas_call(
        lookup_kernel,
        in_specs=[pl.BlockSpec(memory_space=pltpu.HBM)] * 4,
        out_specs=pl.BlockSpec(memory_space=pltpu.VMEM),
        out_shape=jax.ShapeDtypeStruct((dests, slots // 128, 128), jnp.float32),
        scratch_shapes=[
            pltpu.VMEM((4, rows, cols), jnp.float32),
            pltpu.VMEM((dests, slots // 128, 128), jnp.int32),
            pltpu.VMEM((2 * rows, 128), jnp.int32),
            pltpu.VMEM((256, 4 * rows), jnp.bfloat16),
            pltpu.VMEM((UNROLL, 8, 128), jnp.int32),
            pltpu.VMEM((UNROLL, 8, 128), jnp.float32),
            pltpu.VMEM((8, dests), jnp.int32),
            pltpu.SMEM((8, dests), jnp.int32),
            pltpu.SMEM((dests * (slots // 128) + 8 * UNROLL + 8,), jnp.int32),
            pltpu.SemaphoreType.DMA,
            pltpu.SemaphoreType.DMA((slots // 128 + 4,)),
        ],
        compiler_params=pltpu.CompilerParams(vmem_limit_bytes=53 * 1024 * 1024),
        name="look_up",
    )(moisture, vertical_cond, rain, remap_cell)


HALF_BINS = 64


def step_kernel(
    moist_ref, cond_ref, sent_ref, reach_ref,
    travel_ref, out_before_ref, in_before_ref, outlet_ref,
    moved_ref, flow_ref, inflow_ref,
    edge_rows, edge_cols, pack_up, pack_down, below, above, pack_left, pack_right, from_right, from_left,
    arrived, faces, leave, met, boundary,
    send_sem, recv_sem, row_send, row_recv, col_send, col_recv, own_sem, leave_send, leave_recv,
):
    n_row, n_col = lax.axis_size("row"), lax.axis_size("col")
    devices = n_row * n_col
    my_row, my_col = lax.axis_index("row"), lax.axis_index("col")
    me = my_row * n_col + my_col
    layers, rows, cols = moist_ref.shape
    height, width = rows + 8, cols + 128
    fields = (moist_ref, cond_ref)

    barrier = pltpu.get_barrier_semaphore()

    def wrap(x, size):
        return jnp.where(x >= size, x - size, x)

    ahead = [wrap(my_col + dc, n_col) for dc in range(n_col)]
    behind = [wrap(my_col + n_col - dc, n_col) for dc in range(n_col)]

    def greet(dr, first):
        row = wrap(my_row + dr, n_row)
        for dc in range(first, n_col):
            pl.semaphore_signal(
                barrier, inc=1, device_id=(row, ahead[dc]), device_id_type=MESH
            )

    greet(0, 1)

    @pl.loop(1, n_row)
    def _(dr):
        greet(dr, 0)

    travel = travel_ref[...]
    denom = 1.0 / (1.0 + 2.0 * travel * (1.0 - WEIGHT_X))
    gain = (1.0 - 2.0 * travel * WEIGHT_X) * denom
    rest = (1.0 + 2.0 * travel * WEIGHT_X) * denom * in_before_ref[...]
    rest += (2.0 * travel * (1.0 - WEIGHT_X) - 1.0) * denom * out_before_ref[...]

    has_up, has_down = my_row > 0, my_row < n_row - 1
    has_left, has_right = my_col > 0, my_col < n_col - 1

    sub = lax.broadcasted_iota(jnp.int32, (layers, 8, cols), 1)
    pack_up[...] = jnp.where(
        sub < SUB, moist_ref[:, 0:8, :], pltpu.roll(cond_ref[:, 0:8, :], 8 - SUB, 1)
    )
    pack_down[...] = jnp.where(
        sub >= 8 - SUB,
        moist_ref[:, rows - 8 : rows, :],
        pltpu.roll(cond_ref[:, rows - 8 : rows, :], SUB, 1),
    )

    def row_copy(up):
        return pltpu.make_async_remote_copy(
            src_ref=pack_up if up else pack_down,
            dst_ref=below if up else above,
            send_sem=row_send.at[0 if up else 1],
            recv_sem=row_recv.at[0 if up else 1],
            device_id=(my_row - 1 if up else my_row + 1, my_col),
            device_id_type=MESH,
        )

    pl.semaphore_wait(barrier, devices - 1)

    def send_lists(dr, first):
        row = wrap(my_row + dr, n_row)
        for dc in range(first, n_col):
            pltpu.make_async_remote_copy(
                src_ref=sent_ref.at[row * n_col + ahead[dc]],
                dst_ref=arrived.at[dr * n_col + dc],
                send_sem=send_sem,
                recv_sem=recv_sem.at[dr],
                device_id=(row, ahead[dc]),
                device_id_type=MESH,
            ).start()

    send_lists(0, 1)

    @pl.loop(1, n_row)
    def _(dr):
        send_lists(dr, 0)

    def lists_wait(sem, first, count):
        place = arrived.at[pl.ds(first, count)]
        pltpu.make_async_copy(place, place, sem).wait()

    @pl.when(has_up)
    def _():
        row_copy(True).start()

    @pl.when(has_down)
    def _():
        row_copy(False).start()

    own = pltpu.make_async_copy(sent_ref.at[me], arrived.at[0], own_sem)
    own.start()

    def face(c, axis):
        size = c.shape[axis]
        near = pltpu.roll(c, size - 1, axis)
        return 2.0 * c * near / jnp.maximum(c + near, 1e-30)

    def inner_faces(l, carry):
        c = cond_ref[l]
        faces[0, l] = face(c, 0)
        faces[1, l] = face(c, 1)
        return carry

    lax.fori_loop(0, layers, inner_faces, 0)

    own.wait()
    base = lax.broadcasted_iota(jnp.int32, (16, 1024), 0).astype(jnp.float32).astype(jnp.bfloat16)
    zero = jnp.zeros((16, 1024), jnp.bfloat16)
    one = jnp.ones((16, 1024), jnp.bfloat16)

    def spread(x):
        return jnp.concatenate(
            [jnp.broadcast_to(x[j : j + 1, :], (16, 128)).astype(jnp.bfloat16) for j in range(8)], 1
        )

    def add_up(dr, acc):
        row = wrap(my_row + n_row - dr, n_row)
        for dc in range(n_col):
            k = dr * n_col + dc
            q = reach_ref[row * n_col + behind[dc]]
            value = arrived[k]
            first = value.astype(jnp.bfloat16).astype(jnp.float32)
            head, tail = spread(first), spread(value - first)
            a = spread(((q >> 7) + 16 * ((q >> 6) & 1)).astype(jnp.float32))
            b = spread((q & 63).astype(jnp.float32))
            hits = [base + jnp.bfloat16(16 * t) == a for t in range(2)]
            values = jnp.concatenate(
                [jnp.where(h, head, zero) for h in hits] + [jnp.where(h, tail, zero) for h in hits], 0
            )
            places = jnp.concatenate(
                [jnp.where(base + jnp.bfloat16(16 * t) == b, one, zero) for t in range(4)], 0
            )
            acc = acc + lax.dot_general(values, places, NT, preferred_element_type=jnp.float32)
        return acc

    def wait_and_add(dr, acc):
        lists_wait(recv_sem.at[dr], dr * n_col, n_col)
        return add_up(dr, acc)

    lists_wait(recv_sem.at[0], 1, n_col - 1)
    bins = add_up(0, jnp.zeros((64, HALF_BINS), jnp.float32))
    bins = lax.fori_loop(1, n_row // 2, wait_and_add, bins)

    edge_rows[...] = jnp.zeros_like(edge_rows)

    @pl.when(has_down)
    def _():
        row_copy(True).wait_recv()
        edge_rows[0] = jnp.where(sub < SUB, below[...], 0.0)
        edge_rows[1] = jnp.where(sub < SUB, pltpu.roll(below[...], SUB, 1), 0.0)

    @pl.when(has_up)
    def _():
        row_copy(False).wait_recv()
        edge_rows[0] = jnp.where(sub >= 8 - SUB, above[...], edge_rows[0])
        edge_rows[1] = jnp.where(sub >= 8 - SUB, pltpu.roll(above[...], 8 - SUB, 1), edge_rows[1])

    def tall(f, l, lanes):
        return jnp.concatenate([fields[f][l, :, lanes], edge_rows[f, l, :, lanes]], 0)

    lane = lax.broadcasted_iota(jnp.int32, (height, 128), 1)
    left_pack = jnp.zeros((height, 128), jnp.float32)
    right_pack = jnp.zeros((height, 128), jnp.float32)
    for p in range(2 * layers):
        here = (lane >= SUB * p) & (lane < SUB * (p + 1))
        first = tall(p // layers, p % layers, slice(0, 128))
        last = tall(p // layers, p % layers, slice(cols - 128, cols))
        left_pack = jnp.where(here, pltpu.roll(first, SUB * p, 1) if p else first, left_pack)
        right_pack = jnp.where(here, pltpu.roll(last, SUB * p + SUB, 1), right_pack)
    pack_left[...] = left_pack
    pack_right[...] = right_pack

    def col_copy(left):
        return pltpu.make_async_remote_copy(
            src_ref=pack_left if left else pack_right,
            dst_ref=from_right if left else from_left,
            send_sem=col_send.at[0 if left else 1],
            recv_sem=col_recv.at[0 if left else 1],
            device_id=(my_row, my_col - 1 if left else my_col + 1),
            device_id_type=MESH,
        )

    @pl.when(has_left)
    def _():
        col_copy(True).start()

    @pl.when(has_right)
    def _():
        col_copy(False).start()

    bins = lax.fori_loop(n_row // 2, n_row, wait_and_add, bins)
    bins = SIDEWAYS_FACTOR * (bins[0:32] + bins[32:64])
    lateral_flow = jnp.concatenate([bins[0:16], bins[16:32]], 1)

    segments = lateral_flow.shape[0]
    offset_term = gain * lateral_flow + rest
    gains, offsets = [gain[0:1]], [offset_term[0:1]]
    for i in range(1, segments):
        g = gain[i : i + 1]
        gains.append(g * gains[-1])
        offsets.append(g * offsets[-1] + offset_term[i : i + 1])

    leave[0:1] = gains[-1]
    leave[1:2] = offsets[-1]
    leave[2:3] = outlet_ref[...].astype(jnp.float32)
    leave[3:8] = jnp.zeros((5, leave.shape[1]), jnp.float32)

    def leave_copy(d):
        return pltpu.make_async_remote_copy(
            src_ref=leave,
            dst_ref=met.at[d],
            send_sem=leave_send.at[d],
            recv_sem=leave_recv.at[d],
            device_id=(my_row + d, my_col),
            device_id_type=MESH,
        )

    for d in range(1, n_row):

        @pl.when(my_row + d < n_row)
        def _():
            leave_copy(d).start()

    edge_cols[...] = jnp.zeros_like(edge_cols)

    @pl.when(has_right)
    def _():
        col_copy(True).wait_recv()
        packed = from_right[...]
        for p in range(2 * layers):
            part = pltpu.roll(packed, 128 - SUB * p, 1) if p else packed
            edge_cols[p // layers, p % layers] = jnp.where(lane < SUB, part, 0.0)

    @pl.when(has_left)
    def _():
        col_copy(False).wait_recv()
        packed = from_left[...]
        for p in range(2 * layers):
            part = pltpu.roll(packed, 128 - SUB - SUB * p, 1)
            edge_cols[p // layers, p % layers] = jnp.where(
                lane >= 128 - SUB, part, edge_cols[p // layers, p % layers]
            )

    def lateral(l, carry):
        m = jnp.concatenate([tall(0, l, slice(0, cols)), edge_cols[0, l]], 1)
        last, edge, side = cond_ref[l, rows - 8 : rows, :], edge_rows[1, l], edge_cols[1, l]
        strip = jnp.concatenate([last, edge, cond_ref[l, 0:8, :]], 0)
        low = jnp.concatenate([faces[0, l, 0 : rows - 8, :], face(strip, 0)[0:16]], 0)
        face_down = jnp.concatenate([low, face(side, 0)], 1)
        strip = jnp.concatenate(
            [cond_ref[l, :, cols - 128 : cols], side[0:rows], cond_ref[l, :, 0:128]], 1
        )
        wide = jnp.concatenate([faces[1, l, :, 0 : cols - 128], face(strip, 1)[:, 0:256]], 1)
        face_right = jnp.concatenate([wide, face(jnp.concatenate([edge, side[rows:]], 1), 1)], 0)
        for _ in range(SUB):
            flux_down = face_down * (pltpu.roll(m, height - 1, 0) - m)
            flux_right = face_right * (pltpu.roll(m, width - 1, 1) - m)
            m = m + (
                (flux_down - pltpu.roll(flux_down, 1, 0))
                + (flux_right - pltpu.roll(flux_right, 1, 1))
            )
        moved_ref[l] = m[0:rows, 0:cols]
        return carry

    lax.fori_loop(0, layers, lateral, 0, unroll=2)

    boundary[...] = jnp.zeros_like(boundary)
    reach_lane = lax.broadcasted_iota(jnp.int32, (128, 128), 0).astype(jnp.float32)
    row16 = lax.broadcasted_iota(jnp.int32, (16, 128), 0)
    for d in range(n_row - 1, 0, -1):

        @pl.when(my_row >= d)
        def _():
            leave_copy(d).wait_recv()
            block = met[d]
            goal = jnp.where(reach_lane == block[2:3], 1.0, 0.0).astype(jnp.bfloat16)
            flow = jnp.broadcast_to(block[0:1] * boundary[0:1] + block[1:2], (16, 128))
            first = flow.astype(jnp.bfloat16).astype(jnp.float32)
            second = (flow - first).astype(jnp.bfloat16).astype(jnp.float32)
            third = flow - first - second
            pieces = jnp.where(
                row16 == 0, first, jnp.where(row16 == 1, second, jnp.where(row16 == 2, third, 0.0))
            ).astype(jnp.bfloat16)
            got = lax.dot_general(pieces, goal, NT, preferred_element_type=jnp.float32)
            boundary[0:1] = got[0:1] + got[1:2] + got[2:3]

    enter = boundary[0:1]
    flows = [gains[i] * enter + offsets[i] for i in range(segments)]
    flow_ref[...] = jnp.concatenate(flows, 0)
    inflow_ref[...] = jnp.concatenate([enter] + flows[:-1], 0) + lateral_flow

    lists_wait(send_sem, 1, devices - 1)

    @pl.when(has_up)
    def _():
        row_copy(True).wait_send()

    @pl.when(has_down)
    def _():
        row_copy(False).wait_send()

    @pl.when(has_left)
    def _():
        col_copy(True).wait_send()

    @pl.when(has_right)
    def _():
        col_copy(False).wait_send()

    for d in range(1, n_row):

        @pl.when(my_row + d < n_row)
        def _():
            leave_copy(d).wait_send()


def exchange_step(moisture, lateral_cond, sent, reach, travel, out_b, in_b, outlet):
    layers, rows, cols = moisture.shape
    devices = sent.shape[0]
    n_row = lax.axis_size("row")
    height = rows + 8
    f32 = jnp.float32
    vmem = pl.BlockSpec(memory_space=pltpu.VMEM)
    dma = pltpu.SemaphoreType.DMA
    return pl.pallas_call(
        step_kernel,
        in_specs=[vmem] * 8,
        out_specs=[vmem] * 3,
        out_shape=[
            jax.ShapeDtypeStruct(moisture.shape, f32),
            jax.ShapeDtypeStruct(travel.shape, f32),
            jax.ShapeDtypeStruct(travel.shape, f32),
        ],
        scratch_shapes=[
            pltpu.VMEM((2, layers, 8, cols), f32),
            pltpu.VMEM((2, layers, height, 128), f32),
            pltpu.VMEM((layers, 8, cols), f32),
            pltpu.VMEM((layers, 8, cols), f32),
            pltpu.VMEM((layers, 8, cols), f32),
            pltpu.VMEM((layers, 8, cols), f32),
            pltpu.VMEM((height, 128), f32),
            pltpu.VMEM((height, 128), f32),
            pltpu.VMEM((height, 128), f32),
            pltpu.VMEM((height, 128), f32),
            pltpu.VMEM((devices, 8, 128), f32),
            pltpu.VMEM((2, layers, rows, cols), f32),
            pltpu.VMEM((8, 128), f32),
            pltpu.VMEM((n_row, 8, 128), f32),
            pltpu.VMEM((8, 128), f32),
            dma,
            dma((n_row,)),
            dma((2,)),
            dma((2,)),
            dma((2,)),
            dma((2,)),
            dma,
            dma((n_row,)),
            dma((n_row,)),
        ],
        compiler_params=pltpu.CompilerParams(
            collective_id=0, has_side_effects=True, vmem_limit_bytes=24 * 1024 * 1024
        ),
        name="exchange_step",
    )(moisture, lateral_cond, sent, reach, travel, out_b, in_b, outlet)


def finish_kernel(
    moved_ref, vert_ref, rain_ref, moist_ref, flow_in_ref, inflow_in_ref,
    new_ref, flow_ref, inflow_ref,
    solved, new_sem, flow_sem,
):
    layers, rows, _ = moved_ref.shape
    steps = rows // 8
    flow_copies = [
        pltpu.make_async_copy(flow_in_ref, flow_ref, flow_sem.at[0]),
        pltpu.make_async_copy(inflow_in_ref, inflow_ref, flow_sem.at[1]),
    ]
    for copy in flow_copies:
        copy.start()

    def new_copy(i):
        at = pl.ds(pl.multiple_of(i * 8, 8), 8)
        return pltpu.make_async_copy(solved.at[:, at, :], new_ref.at[:, at, :], new_sem.at[i])

    def solve(i, carry):
        at = pl.ds(pl.multiple_of(i * 8, 8), 8)
        upper, value = [], []
        for l in range(layers):
            v = vert_ref[l, at, :]
            right = moved_ref[l, at, :]
            if l == 0:
                wet = moist_ref[0, at, :]
                right = right + (rain_ref[at, :] - rain_ref[at, :] * (4.0 * wet * wet))
                diag = 1.0 + v
            else:
                diag = 1.0 + v + above * (1.0 - upper[-1])
                right = right + above * value[-1]
            inverse = 1.0 / diag
            upper.append(v * inverse)
            value.append(right * inverse)
            above = v
        x = value[-1]
        solved[layers - 1, at, :] = x
        for l in range(layers - 2, -1, -1):
            x = value[l] + upper[l] * x
            solved[l, at, :] = x
        new_copy(i).start()
        return carry

    lax.fori_loop(0, steps, solve, 0, unroll=2)
    for copy in flow_copies:
        copy.wait()
    for i in range(steps):
        new_copy(i).wait()


def finish(moved, vertical_cond, rain, moisture, flow, inflow):
    vmem = pl.BlockSpec(memory_space=pltpu.VMEM)
    out = pl.BlockSpec(memory_space=pl.ANY)
    return pl.pallas_call(
        finish_kernel,
        in_specs=[vmem] * 6,
        out_specs=[out] * 3,
        out_shape=[
            jax.ShapeDtypeStruct(moved.shape, jnp.float32),
            jax.ShapeDtypeStruct(flow.shape, jnp.float32),
            jax.ShapeDtypeStruct(flow.shape, jnp.float32),
        ],
        scratch_shapes=[
            pltpu.VMEM(moved.shape, jnp.float32),
            pltpu.SemaphoreType.DMA((moved.shape[1] // 8,)),
            pltpu.SemaphoreType.DMA((2,)),
        ],
        compiler_params=pltpu.CompilerParams(vmem_limit_bytes=16 * 1024 * 1024),
        name="finish",
    )(moved, vertical_cond, rain, moisture, flow, inflow)


def shards(
    moisture,
    lateral_cond,
    vertical_cond,
    rain,
    remap_cell,
    remap_reach,
    travel_time,
    outflow_before,
    inflow_before,
    outlet_lane,
):
    sent = look_up(moisture, vertical_cond, rain, remap_cell)
    reach = remap_reach.reshape(sent.shape)
    moved, flow, inflow = exchange_step(
        moisture, lateral_cond, sent, reach, travel_time, outflow_before, inflow_before, outlet_lane
    )
    return tuple(finish(moved, vertical_cond, rain, moisture, flow, inflow))


def solution(mesh):
    in_specs = (
        P(None, "row", "col"),
        P(None, "row", "col"),
        P(None, "row", "col"),
        P("row", "col"),
        P(("row", "col"), None, None),
        P(None, ("row", "col"), None),
        P("row", "col"),
        P("row", "col"),
        P("row", "col"),
        P("row", "col"),
    )
    out_specs = (P(None, "row", "col"), P("row", "col"), P("row", "col"))
    return jax.shard_map(shards, mesh=mesh, in_specs=in_specs, out_specs=out_specs, check_vma=False)
```
